32 devices in a mesh: groups: 2 (over y), slab: 4 (over z), chan: 4 (over x, core).
Axes of the slice: x: 2, y: 2, z: 4, core: 2. Of those that a mesh axis runs over, the one named last changes fastest.
Arguments:
- field: bfloat16 [8, 32, 128, 128, 128], P(('groups', 'chan'), None, 'slab'), parts along dimension 0, may hold values from -6 to 6
- cotangent: bfloat16 [8, 32, 128, 128, 128], P(('groups', 'chan'), None, 'slab'), parts along dimension 0, may hold values from -6 to 6
- spec_weight: bfloat16 [2, 16, 128, 32, 32], P(None, None, 'slab'), may hold values from -1 to 1
- point_weight: bfloat16 [32, 32], replicated, may hold values from -1 to 1
- bias: float32 [32], replicated, may hold values from -4 to 4
Outputs:
- field_grad: bfloat16 [8, 32, 128, 128, 128], P(('groups', 'chan'), None, 'slab'), parts along dimension 0
- spec_grad: float32 [4, 16, 128, 32, 32], P('groups', None, 'slab'), parts along dimension 0
- point_grad: float32 [64, 32], P('groups'), parts along dimension 0
- bias_grad: float32 [64], P('groups'), parts along dimension 0
The draws below stay inside these ranges and needn't reach their ends.
There are 2 independent parts, one for each index of `groups`. The reference program is written for one: setup_inputs(seed, part) draws one part's arguments, and reference() takes and returns one part's arrays. A program takes and returns all parts, laid end to end along the dimension named above; an argument that names none is the same for every part. Nothing has to cross between parts.
All inputs are finite; a program needn't handle non-finite values.
Results may differ from the reference program's by a relative error of at most 0.0061.
Values sent between devices are 32-bit elements; how exact they have to be, the bound alone decides.
No kernel may reach another device: no remote copies, remote signals or barrier semaphores. Data moves between devices by JAX's collectives and lax.ppermute only.
A program may use at most 448 MiB of HBM per device.

```python
import math
import jax
import jax.numpy as jnp
from jax import lax

C = 32
NX = 128
NY = 128
NZ = 128
MX = 16
MY = 16
MZ = 8
K = 128
SAMPLES = 4


def levels(own_key, shape, cuts, smallest, high):
    def one(axis_at, blocks):
        steps = jax.random.uniform(jax.random.fold_in(jax.random.fold_in(own_key, 6), axis_at), (blocks,), jnp.float32, smallest / len(cuts), high / len(cuts))
        return jnp.repeat(jnp.exp(steps), shape[axis_at] // blocks).reshape((-1,) + (1,) * (len(shape) - axis_at - 1))

    level = one(*cuts[0])
    for cut in cuts[1:]:
        level = level * one(*cut)
    return level


def gaussian(key, dims, spread, most, split=(), held_as=jnp.bfloat16):
    entries = spread * jax.random.normal(key, dims, jnp.float32)
    if split:
        entries = entries * levels(key, dims, split, -0.22, 0.18)
    return jnp.clip(entries, -most, most).astype(held_as)


def setup_inputs(seed: int = 0, part: int = 0) -> dict:
    key_of = jax.random.split(jax.random.key(seed), 6)
    part_keys = jax.random.split(jax.random.fold_in(key_of[5], part), 6)
    return {
        "field": gaussian(part_keys[0], (SAMPLES, C, NX, NY, NZ), 1.0, 6.0, ((0, 4), (2, 4))),
        "cotangent": gaussian(part_keys[1], (SAMPLES, C, NX, NY, NZ), 1.0, 6.0, ((0, 4), (2, 4))),
        "spec_weight": gaussian(key_of[2], (2, MX, K, C, C), C ** -0.5, 1.0, ((2, 4),)),
        "point_weight": gaussian(key_of[3], (C, C), C ** -0.5, 1.0),
        "bias": gaussian(key_of[4], (C,), 1.0, 4.0, (), jnp.float32),
    }


highest = lax.Precision.HIGHEST

def contract(form, left, right):
    return jnp.einsum(form, left, right, precision=highest)

def mode_tables(length, count_modes, signed):
    position = jnp.arange(length, dtype=jnp.int32)[:, None]
    mode_index = jnp.arange(count_modes, dtype=jnp.int32)[None, :]
    if signed:
        frequency = jnp.where(mode_index >= count_modes // 2, mode_index - count_modes, mode_index)
    else:
        frequency = mode_index
    phase = position * frequency % length
    phase_angle = phase.astype(jnp.float32) * (2.0 * math.pi / length)
    return (jnp.cos(phase_angle), -jnp.sin(phase_angle))

def gelu_slope(value):
    inner = 0.7978845608 * (value + 0.044715 * value * value * value)
    tanh_value = jnp.tanh(inner)
    return 0.5 * (1.0 + tanh_value) + 0.5 * value * (1.0 - tanh_value * tanh_value) * 0.7978845608 * (1.0 + 0.134145 * value * value)

def spectrum(field_one, tables):
    ycos, ysin, zcos, zsin, xcos, xsin = tables
    values = field_one.astype(jnp.float32)
    q_real = contract('cxyz,yk->cxkz', values, ycos.astype(jnp.float32))
    q_imag = contract('cxyz,yk->cxkz', values, ysin.astype(jnp.float32))
    r_real = contract('cxkz,zj->cxkj', q_real, zcos) - contract('cxkz,zj->cxkj', q_imag, zsin)
    r_imag = contract('cxkz,zj->cxkj', q_real, zsin) + contract('cxkz,zj->cxkj', q_imag, zcos)
    r_real = r_real.reshape(C, NX, MY * MZ)
    r_imag = r_imag.reshape(C, NX, MY * MZ)
    u_real = contract('cxk,xm->cmk', r_real, xcos) - contract('cxk,xm->cmk', r_imag, xsin)
    u_imag = contract('cxk,xm->cmk', r_imag, xcos) + contract('cxk,xm->cmk', r_real, xsin)
    return jnp.stack([u_real, u_imag]) * (1.0 / math.sqrt(NX * NY * NZ))

def inverse(spectra, tables):
    ycos, ysin, zcos, zsin, xcos, xsin = tables
    h_real, h_imag = (spectra[0], spectra[1])
    b_real = contract('cmk,xm->cxk', h_real, xcos) + contract('cmk,xm->cxk', h_imag, xsin)
    b_imag = contract('cmk,xm->cxk', h_imag, xcos) - contract('cmk,xm->cxk', h_real, xsin)
    b_real = b_real.reshape(C, NX, MY, MZ)
    b_imag = b_imag.reshape(C, NX, MY, MZ)
    f_real = contract('cxkj,zj->cxkz', b_real, zcos) + contract('cxkj,zj->cxkz', b_imag, zsin)
    f_imag = contract('cxkj,zj->cxkz', b_imag, zcos) - contract('cxkj,zj->cxkz', b_real, zsin)
    f_real = lax.optimization_barrier(f_real.astype(jnp.bfloat16)).astype(jnp.float32)
    f_imag = lax.optimization_barrier(f_imag.astype(jnp.bfloat16)).astype(jnp.float32)
    result = contract('cxkz,yk->cxyz', f_real, ycos.astype(jnp.float32)) + contract('cxkz,yk->cxyz', f_imag, ysin.astype(jnp.float32))
    return result * (1.0 / math.sqrt(MX * MY * MZ))

def mix_forward(spectra, weights):
    w_real, w_imag = (weights[0], weights[1])
    u_real, u_imag = (spectra[0], spectra[1])
    v_real = contract('cmk,mkco->omk', u_real, w_real) - contract('cmk,mkco->omk', u_imag, w_imag)
    v_imag = contract('cmk,mkco->omk', u_imag, w_real) + contract('cmk,mkco->omk', u_real, w_imag)
    return jnp.stack([v_real, v_imag])

def mix_adjoint(spectra, weights):
    w_real, w_imag = (weights[0], weights[1])
    g_real, g_imag = (spectra[0], spectra[1])
    h_real = contract('omk,mkco->cmk', g_real, w_real) + contract('omk,mkco->cmk', g_imag, w_imag)
    h_imag = contract('omk,mkco->cmk', g_imag, w_real) - contract('omk,mkco->cmk', g_real, w_imag)
    return jnp.stack([h_real, h_imag])

def reference(field, cotangent, spec_weight, point_weight, bias):
    ycos, ysin = mode_tables(NY, MY, True)
    zcos, zsin = mode_tables(NZ, MZ, False)
    xcos, xsin = mode_tables(NX, MX, True)
    tables = (ycos.astype(jnp.bfloat16), ysin.astype(jnp.bfloat16), zcos, zsin, xcos, xsin)
    weights = spec_weight.astype(jnp.float32)
    point32 = point_weight.astype(jnp.float32)

    def one_sample(pair):
        field_one, cot_one = pair
        values = field_one.astype(jnp.float32)
        uhat = spectrum(field_one, tables)
        vhat = mix_forward(uhat, weights)
        pre = inverse(vhat, tables) + contract('co,cxyz->oxyz', point32, values) + bias[:, None, None, None]
        dpre = (cot_one.astype(jnp.float32) * gelu_slope(pre)).astype(jnp.bfloat16)
        dpre32 = dpre.astype(jnp.float32)
        ghat = spectrum(dpre, tables)
        hhat = mix_adjoint(ghat, weights)
        grad_one = inverse(hhat, tables) + contract('co,oxyz->cxyz', point32, dpre32)
        dw_real = contract('cmk,omk->mkco', uhat[0], ghat[0]) + contract('cmk,omk->mkco', uhat[1], ghat[1])
        dw_imag = contract('cmk,omk->mkco', uhat[0], ghat[1]) - contract('cmk,omk->mkco', uhat[1], ghat[0])
        point_part = contract('cxyz,oxyz->co', values, dpre32)
        bias_part = lax.optimization_barrier(jnp.sum(dpre32, axis=(1, 2, 3)))
        return (grad_one.astype(jnp.bfloat16), jnp.stack([dw_real, dw_imag]), point_part, bias_part)
    grads, weight_parts, point_parts, bias_parts = lax.map(one_sample, (field, cotangent))
    norm_scale = 1.0 / math.sqrt(SAMPLES * NX * NY * NZ)
    spec_grad = lax.optimization_barrier(jnp.sum(weight_parts, axis=0))
    point_grad = lax.optimization_barrier(jnp.sum(point_parts, axis=0)) * norm_scale
    bias_grad = lax.optimization_barrier(jnp.sum(bias_parts, axis=0)) * norm_scale
    return (grads, spec_grad, point_grad, bias_grad)
```

```python
import functools
import math

import jax
import jax.numpy as jnp
import numpy as np
from jax import lax
from jax.experimental import pallas as pl
from jax.experimental.pallas import tpu as pltpu
from jax.sharding import PartitionSpec as P

NX = 128
NY = 128
NZ = 128
MX = 16
MY = 16
MZ = 8
LANES = 128
GROUP = 8

FIELD_CB = 4
GRAD_CB = 2

f32 = jnp.float32
bf16 = jnp.bfloat16

GA = 0.7978845608
GB = 0.044715
GK = (GA * GB) ** (1.0 / 3.0)
GALPHA = GA / GK

SCALE_FORWARD = 1.0 / math.sqrt(NX * NY * NZ)
SCALE_INVERSE = 1.0 / math.sqrt(MX * MY * MZ)


def mode_table(length, count, signed):
    position = np.arange(length)[:, None]
    index = np.arange(count)[None, :]
    frequency = np.where(index >= count // 2, index - count, index) if signed else index
    angle = (position * frequency % length).astype(np.float64) * (2.0 * math.pi / length)
    return np.cos(angle).astype(np.float32), (-np.sin(angle)).astype(np.float32)


def bf(value):
    return np.asarray(value, np.float32).astype(jnp.bfloat16)


def split_bf(value):
    high = bf(value)
    return high, bf(np.asarray(value, np.float32) - high.astype(np.float32))


def z_forward_table():
    zc, zs = mode_table(NZ, MZ, False)
    block = np.concatenate([zc, zs], axis=1)
    table = np.zeros((GROUP, NZ, GROUP, 2 * MZ), np.float32)
    for x in range(GROUP):
        table[x, :, x] = block
    return bf(table.reshape(GROUP * NZ, GROUP * 2 * MZ))


def z_inverse_table():
    zc, zs = mode_table(NZ, MZ, False)
    block = np.concatenate([zc, zs], axis=1).T
    table = np.zeros((GROUP // 2, GROUP, 2 * MZ, 2, NZ), np.float32)
    for x in range(GROUP):
        table[x // 2, x, :, x % 2] = block
    return bf(table.reshape(GROUP // 2, GROUP * 2 * MZ, 2 * NZ))


def y_tables():
    yc, ys = mode_table(NY, MY, True)
    forward = np.concatenate([yc.T, ys.T], axis=0)
    inverse = np.concatenate([yc, ys, yc, ys], axis=1)
    return bf(forward), bf(inverse)


def x_forward_table():
    xc, xs = mode_table(NX, MX, True)
    table = np.zeros((NX, 2, MZ, 2, MX, MZ), np.float32)
    for kz in range(MZ):
        table[:, 0, kz, 0, :, kz] = xc
        table[:, 1, kz, 0, :, kz] = -xs
        table[:, 0, kz, 1, :, kz] = xs
        table[:, 1, kz, 1, :, kz] = xc
    return table.reshape(NX * 2 * MZ, 2 * MX * MZ) * SCALE_FORWARD


def x_inverse_table(scale, ns):
    xc, xs = mode_table(NX, MX, True)
    table = np.zeros((2, MX, MZ, 2, NX, 2, MZ), np.float32)
    for kz in range(MZ):
        re_re, im_re = xc.T, xs.T
        re_im, im_im = -xs.T, xc.T
        table[0, :, kz, 0, :, 0, kz] = re_re
        table[1, :, kz, 0, :, 0, kz] = im_re
        table[0, :, kz, 0, :, 1, kz] = re_im
        table[1, :, kz, 0, :, 1, kz] = im_im
        table[0, :, kz, 1, :, 0, kz] = re_im
        table[1, :, kz, 1, :, 0, kz] = im_im
        table[0, :, kz, 1, :, 1, kz] = -re_re
        table[1, :, kz, 1, :, 1, kz] = -im_re
    table = table.reshape(2 * MX * MZ, 2, ns, NX // ns * 2 * MZ).transpose(2, 0, 1, 3)
    return table.reshape(ns, 2 * MX * MZ, -1) * scale


def dot(a, b):
    return jnp.dot(a, b, preferred_element_type=f32)


def parts(value):
    high = value.astype(bf16)
    return high, (value - high.astype(f32)).astype(bf16)


def dot3(a, bh, bl):
    ah, al = parts(a)
    return dot(ah, bh) + dot(al, bh) + dot(ah, bl)


def z_forward(tiles, zf):
    wide = jnp.concatenate(
        [
            jnp.concatenate(tiles[g : g + GROUP], axis=1)
            for g in range(0, len(tiles), GROUP)
        ],
        axis=0,
    )
    q = dot(wide, zf).astype(bf16)
    return [q[g : g + NY] for g in range(0, q.shape[0], NY)]


def y_forward(groups, yf):
    r = dot(yf, jnp.concatenate(groups, axis=1))
    top, bot = r[:MY], r[MY:]
    lanes = bot.shape[1]
    at = lax.broadcasted_iota(jnp.int32, top.shape, 1) % (2 * MZ)
    return jnp.where(
        at < MZ, top - pltpu.roll(bot, lanes - MZ, 1), top + pltpu.roll(bot, MZ, 1)
    )


def x_forward_out(me, ns, channels, r_scr, xfh, xfl, outs):
    rows = (MY // ns) * channels
    r = jnp.concatenate([r_scr[i] for i in range(r_scr.shape[0])], axis=1)
    width = xfh.shape[1]
    done = dot3(r, xfh[...], xfl[...])
    for i in range(width // LANES):
        r_scr[i] = done[:, i * LANES : (i + 1) * LANES]
    for k in range(ns):
        owner = lax.rem(me + k, ns)
        at = pl.ds(pl.multiple_of(owner * rows, rows), rows)
        for i in range(width // LANES):
            outs[k][:, :, i * LANES : (i + 1) * LANES] = r_scr[i, at, :].reshape(
                MY // ns, channels, LANES
            )


def x_inverse_in(me, ns, channels, ins, xih, xil, b_scr):
    rows = (MY // ns) * channels
    for k in range(ns):
        owner = lax.rem(me + ns - k, ns)
        h = ins[k][...].reshape(rows, -1)
        b = dot3(h, xih[0], xil[0])
        for i in range(b_scr.shape[0]):
            at = pl.ds(pl.multiple_of(owner * rows, rows), rows)
            b_scr[i, at, :] = b[:, i * LANES : (i + 1) * LANES]


def put_channel(scr, c, channels, value):
    for i in range(scr.shape[0]):
        scr[i, pl.ds(c, MY, stride=channels), :] = value[:, i * LANES : (i + 1) * LANES]


def get_channel(scr, c, channels, blocks):
    return jnp.concatenate(
        [scr[i, pl.ds(c, MY, stride=channels), :] for i in blocks], axis=1
    )


def y_inverse(bs, yi):
    lanes = bs[0].shape[1] // 2
    rhs = []
    for b in bs:
        high, low = parts(b)
        rhs.append(
            jnp.concatenate(
                [high[:, :lanes], high[:, lanes:], low[:, :lanes], low[:, lanes:]], axis=0
            )
        )
    return dot(yi, jnp.concatenate(rhs, axis=1)).astype(bf16)


def kron_halves(block):
    channels, _, lanes = block.shape
    wide = block.astype(f32).reshape(channels, 2, 8, lanes)
    return [wide[:, h].reshape(channels * 8, lanes).astype(bf16) for h in range(2)]


def row_pair(ref, y):
    return jnp.concatenate([ref[0, :, 0, y : y + 16, :], ref[0, :, 1, y : y + 16, :]], axis=2)


def whole_rows(value, at, lanes):
    size = value.shape[0] // 8
    two = [value[:, a : a + lanes].reshape(size, 8, lanes) for a in (at, at + lanes)]
    return jnp.concatenate(two, axis=1)


def put_rows(ref, y, value):
    value = value.astype(bf16)
    ref[0, :, 0, y : y + 16, :] = value[:, :, :NZ]
    ref[0, :, 1, y : y + 16, :] = value[:, :, NZ:]


def pick_rows(channels):
    row = lax.broadcasted_iota(jnp.int32, (channels * 8, channels), 0)
    col = lax.broadcasted_iota(jnp.int32, (channels * 8, channels), 1)
    return row // 8 == col


def same_cell(channels):
    size = channels * 8
    row = lax.broadcasted_iota(jnp.int32, (size, size), 0)
    col = lax.broadcasted_iota(jnp.int32, (size, size), 1)
    return row % 8 == col % 8


def kron_rows(point, turned):
    channels = point.shape[0]
    pick = jnp.where(pick_rows(channels), 1.0, 0.0).astype(bf16)
    nt = (((1,), (1,)), ((), ()))
    tn = (((1,), (0,)), ((), ()))
    left = lax.dot_general(pick, point, nt if turned else tn, preferred_element_type=f32)
    full = lax.dot_general(left.astype(bf16), pick, nt, preferred_element_type=f32)
    return jnp.where(same_cell(channels), full, 0.0).astype(bf16)


def field_kernel(ns, channels, me_ref, field, zf, yf, xfh, xfl, *rest):
    outs, r_scr = rest[:ns], rest[ns]
    step = pl.program_id(0)
    rows = field.shape[2]
    lanes = rows * 2 * MZ
    groups = []
    for i in range(FIELD_CB):
        groups += z_forward([field[0, i, x] for x in range(rows)], zf[...])
    spectra = y_forward(groups, yf[...])
    for i in range(FIELD_CB):
        put_channel(r_scr, step * FIELD_CB + i, channels, spectra[:, i * lanes : (i + 1) * lanes])

    @pl.when(step == pl.num_programs(0) - 1)
    def _():
        x_forward_out(me_ref[0], ns, channels, r_scr, xfh, xfl, outs)


def point_kernel(field, point, bias, out, kron):
    channels = field.shape[1]

    @pl.when(pl.program_id(0) == 0)
    def _():
        kron[...] = kron_rows(point[...], True)

    bias_rows = jnp.sum(jnp.where(pick_rows(channels), bias[...], 0.0), axis=1, keepdims=True) * GK
    bias_16 = jnp.concatenate([bias_rows.reshape(channels, 8, 1)] * 2, axis=1)

    halves = []
    for y in range(0, NY, 16):
        halves += kron_halves(row_pair(field, y))
    lanes = halves[0].shape[1]
    done = dot(kron[...], jnp.concatenate(halves, axis=1))
    for y in range(0, NY, 16):
        put_rows(out, y, whole_rows(done, y // 8 * lanes, lanes) * GK + bias_16)


def gelu_slope(v):
    n = v * v
    t = jnp.tanh(v * (n + GALPHA))
    d = v * (1.5 * n + 0.5 * GALPHA)
    return (1.0 + t) * (0.5 + (1.0 - t) * d)


def grad_kernel(ns, channels, me_ref, pre, cot, *rest):
    ins = rest[:ns]
    xih, xil, yi, zi, zf, yf, xfh, xfl = rest[ns : ns + 8]
    dpre = rest[ns + 8]
    outs = rest[ns + 9 : ns + 9 + ns]
    b_scr, r_scr = rest[ns + 9 + ns :]
    step = pl.program_id(0)
    rows = pre.shape[2]
    width = GROUP * 2 * MZ
    groups = rows // GROUP

    @pl.when(step == 0)
    def _():
        x_inverse_in(me_ref[0], ns, channels, ins, xih, xil, b_scr)

    lanes = rows * 2 * MZ
    blocks = range(b_scr.shape[0])
    wide = y_inverse(
        [get_channel(b_scr, step * GRAD_CB + i, channels, blocks) for i in range(GRAD_CB)], yi[...]
    )
    g_all = jnp.concatenate(
        [wide[:, g : g + width] for g in range(0, wide.shape[1], width)], axis=0
    )
    for j in range(GROUP // 2):
        v_all = dot(g_all, zi[j])
        for i in range(GRAD_CB):
            for g in range(groups):
                x = g * GROUP + 2 * j
                at = (i * groups + g) * NY
                v = v_all[at : at + NY]
                v = v + jnp.concatenate([pre[0, i, x], pre[0, i, x + 1]], axis=1).astype(f32)
                w = jnp.concatenate([cot[0, i, x], cot[0, i, x + 1]], axis=1).astype(f32)
                d = (w * gelu_slope(v)).astype(bf16)
                dpre[0, i, x] = d[:, :NZ]
                dpre[0, i, x + 1] = d[:, NZ:]
    done = []
    for i in range(GRAD_CB):
        done += z_forward([dpre[0, i, x] for x in range(rows)], zf[...])
    spectra = y_forward(done, yf[...])
    for i in range(GRAD_CB):
        put_channel(r_scr, step * GRAD_CB + i, channels, spectra[:, i * lanes : (i + 1) * lanes])

    @pl.when(step == pl.num_programs(0) - 1)
    def _():
        x_forward_out(me_ref[0], ns, channels, r_scr, xfh, xfl, outs)


def pair_kernel(field, dpre, out, acc):
    channels = field.shape[1]
    step = pl.program_id(0)

    @pl.when(step == 0)
    def _():
        acc[...] = jnp.zeros_like(acc)

    lefts, rights = [], []
    for y in range(0, NY, 16):
        lefts += kron_halves(row_pair(field, y))
        rights += kron_halves(row_pair(dpre, y))
    acc[...] += lax.dot_general(
        jnp.concatenate(lefts, axis=1),
        jnp.concatenate(rights, axis=1),
        (((1,), (1,)), ((), ())),
        preferred_element_type=f32,
    )

    @pl.when(step == pl.num_programs(0) - 1)
    def _():
        same = jnp.where(same_cell(channels), acc[...], 0.0)
        pick = jnp.where(pick_rows(channels), 1.0, 0.0)
        high = lax.Precision.HIGHEST
        left = jnp.dot(same, pick, precision=high, preferred_element_type=f32)
        out[...] = lax.dot_general(
            pick, left, (((0,), (0,)), ((), ())), precision=high, preferred_element_type=f32
        )


def back_kernel(ns, me_ref, dpre, point, *rest):
    ins = rest[:ns]
    xih, xil, yi, zi = rest[ns : ns + 4]
    out, b_scr, g_scr, kron = rest[ns + 4 :]
    channels = dpre.shape[1]
    step = pl.program_id(0)
    width = GROUP * 2 * MZ

    @pl.when(step == 0)
    def _():
        x_inverse_in(me_ref[0], ns, channels, ins, xih, xil, b_scr)
        kron[...] = kron_rows(point[...], False)

    per_group = GROUP // 2

    @pl.when(step % per_group == 0)
    def _():
        group = step // per_group
        turned = group + b_scr.shape[0] // 2
        wide = y_inverse(
            [get_channel(b_scr, c, channels, (group, turned)) for c in range(channels)], yi[...]
        )
        for c in range(channels):
            g_scr[c] = wide[:, c * width : (c + 1) * width]

    halves = []
    for y in range(0, NY, 16):
        halves += kron_halves(row_pair(dpre, y))
    lanes = halves[0].shape[1]
    point = dot(kron[...], jnp.concatenate(halves, axis=1))
    spec = dot(g_scr[...].reshape(channels * NY, width), zi[step % per_group])
    spec = spec.reshape(channels, NY, lanes)
    for y in range(0, NY, 16):
        put_rows(out, y, whole_rows(point, y // 8 * lanes, lanes) + spec[:, y : y + 16])


def mix_kernel(ns, adjoint, *refs):
    ins, weights, total, out = refs[:ns], refs[ns], refs[ns + 1], refs[ns + 2]
    channels = total.shape[1]
    u = ins[0][...]
    for k in range(1, ns):
        u = u + ins[k][...]
    total[...] = u
    half = total.shape[2] // 2
    if not adjoint:
        real = jnp.zeros((channels, half), f32)
        imag = jnp.zeros((channels, half), f32)
        for c in range(channels):
            a, b = total[0, pl.ds(c, 1), :half], total[0, pl.ds(c, 1), half:]
            wr, wi = weights[0, c, 0].astype(f32), weights[1, c, 0].astype(f32)
            real = real + (wr * a - wi * b)
            imag = imag + (wr * b + wi * a)
        out[0, :, :half] = real
        out[0, :, half:] = imag
    else:
        a, b = total[0, :, :half], total[0, :, half:]
        for c in range(channels):
            wr, wi = weights[0, c, 0].astype(f32), weights[1, c, 0].astype(f32)
            out[0, pl.ds(c, 1), :half] = jnp.sum(wr * a + wi * b, axis=0, keepdims=True)
            out[0, pl.ds(c, 1), half:] = jnp.sum(wr * b - wi * a, axis=0, keepdims=True)


def weight_kernel(weights, out, scr):
    _, kxs, kzs, channels, _ = weights.shape
    modes = kxs * kzs
    scr[:, :channels] = weights[...].astype(f32).reshape(modes * channels, channels)
    per = LANES // channels
    lane = lax.broadcasted_iota(jnp.int32, (modes, LANES), 1) // channels
    for c in range(0, channels, per):
        packed = scr[pl.ds(c, modes, stride=channels), :]
        for q in range(1, per):
            more = scr[pl.ds(c + q, modes, stride=channels), :]
            packed = jnp.where(lane == q, pltpu.roll(more, q * channels, 1), packed)
        turned = packed.T.astype(bf16)
        for q in range(per):
            out[0, c + q, 0] = turned[q * channels : (q + 1) * channels]


def outer_kernel(samples, *refs):
    us, gs, out, scr = refs[:samples], refs[samples : 2 * samples], refs[-2], refs[-1]
    channels = us[0].shape[1]
    modes = us[0].shape[2] // 2
    per = LANES // channels
    tn = (((0,), (0,)), ((), ()))

    def stack(refs):
        wide = jnp.concatenate([ref[0] for ref in refs], axis=1)
        return jnp.concatenate(parts(wide), axis=0)

    def table(lanes, of):
        row = lax.broadcasted_iota(jnp.int32, (2 * channels, lanes), 0) % channels
        col = lax.broadcasted_iota(jnp.int32, (2 * channels, lanes), 1)
        return jnp.where(row == of(col), 1.0, 0.0).astype(bf16)

    by_o = table(LANES, lambda col: col % channels)
    by_c = table(channels * channels, lambda col: col // channels)
    g_all = lax.dot_general(stack(gs), by_o, tn, preferred_element_type=f32)
    u_all = lax.dot_general(stack(us), by_c, tn, preferred_element_type=f32)
    for n in range(channels // per):
        real = imag = None
        for s in range(samples):
            at = 2 * s * modes
            gr, gi = g_all[at : at + modes], g_all[at + modes : at + 2 * modes]
            u = u_all[at : at + 2 * modes, n * LANES : (n + 1) * LANES]
            ur, ui = u[:modes], u[modes:]
            re, im = ur * gr + ui * gi, ur * gi - ui * gr
            real = re if real is None else real + re
            imag = im if imag is None else imag + im
        for p, value in enumerate((real, imag)):
            for q in range(per):
                one = value if q == 0 else pltpu.roll(value, LANES - q * channels, 1)
                scr[p, pl.ds(n * per + q, modes, stride=channels), :] = one
    out[...] = scr[:, :, :channels].reshape(out.shape)


def whole(shape):
    return pl.BlockSpec(shape, lambda *_: (0,) * len(shape))


def params(mib=60, axes=1):
    return pltpu.CompilerParams(
        dimension_semantics=("arbitrary",) * axes, vmem_limit_bytes=mib * 2**20
    )


def make_calls(ns, shape):
    _, channels, rows, _, _ = shape
    own_ky = MY // ns
    width = 2 * MX * MZ
    lanes = rows * 2 * MZ
    size = channels * 8

    zf = jnp.asarray(z_forward_table())
    zi = jnp.asarray(z_inverse_table())
    yf, yi = (jnp.asarray(t) for t in y_tables())
    xf = [jnp.asarray(t) for t in split_bf(x_forward_table())]
    xf_spec = [pl.BlockSpec((lanes, width), lambda i, at: (at[0], 0))] * 2
    xi_pre = [jnp.asarray(t) for t in split_bf(x_inverse_table(SCALE_INVERSE * GK, ns))]
    xi_back = [jnp.asarray(t) for t in split_bf(x_inverse_table(SCALE_INVERSE, ns))]
    xi_spec = [pl.BlockSpec((1, width, 2 * lanes), lambda i, at: (at[0], 0, 0))] * 2

    chunk = jax.ShapeDtypeStruct((own_ky, channels, width), f32)
    chunk_spec = whole(chunk.shape)

    def some_channels(count):
        return pl.BlockSpec((1, count, rows, NY, NZ), lambda c, *_: (0, c, 0, 0, 0))

    two_rows = pl.BlockSpec((1, channels, 2, NY, NZ), lambda x, *_: (0, 0, x, 0, 0))
    big = jax.ShapeDtypeStruct(shape, bf16)
    cells = channels * rows * NY * NZ
    r_scr = pltpu.VMEM((lanes // LANES, MY * channels, LANES), f32)
    b_scr = pltpu.VMEM((2 * lanes // LANES, MY * channels, LANES), f32)
    kron_scr = pltpu.VMEM((size, size), bf16)

    def cost(flops, moved):
        return pl.CostEstimate(flops=int(flops), bytes_accessed=int(moved), transcendentals=0)

    def tables(*arrays):
        return [whole(a.shape) for a in arrays]

    def field_call(me_arr, field):
        return pl.pallas_call(
            functools.partial(field_kernel, ns, channels),
            grid_spec=pltpu.PrefetchScalarGridSpec(
                num_scalar_prefetch=1,
                grid=(channels // FIELD_CB,),
                in_specs=[some_channels(FIELD_CB)] + tables(zf, yf) + xf_spec,
                out_specs=[chunk_spec] * ns,
                scratch_shapes=[r_scr],
            ),
            out_shape=[chunk] * ns,
            compiler_params=params(),
            cost_estimate=cost(cells * 512, cells * 2),
            name="field_spectrum",
        )(me_arr, field, zf, yf, *xf)

    def point_call(field, point_weight, bias):
        return pl.pallas_call(
            point_kernel,
            grid=(rows // 2,),
            in_specs=[two_rows] + tables(point_weight, bias[None]),
            out_specs=two_rows,
            out_shape=big,
            scratch_shapes=[kron_scr],
            compiler_params=params(),
            cost_estimate=cost(cells * 512, cells * 4),
            name="pointwise",
        )(field, point_weight, bias[None])

    def mix_call(adjoint, chunks, w):
        one_ky = pl.BlockSpec((1, channels, width), lambda k: (k, 0, 0))
        w_spec = pl.BlockSpec((2, channels, 1, channels, MX * MZ), lambda k: (0, 0, k, 0, 0))
        return pl.pallas_call(
            functools.partial(mix_kernel, ns, adjoint),
            grid=(own_ky,),
            in_specs=[one_ky] * ns + [w_spec],
            out_specs=[one_ky, one_ky],
            out_shape=[chunk, chunk],
            compiler_params=params(),
            name="mix_adjoint" if adjoint else "mix",
        )(*chunks, w)

    def grad_call(me_arr, pre, cotangent, chunks):
        return pl.pallas_call(
            functools.partial(grad_kernel, ns, channels),
            grid_spec=pltpu.PrefetchScalarGridSpec(
                num_scalar_prefetch=1,
                grid=(channels // GRAD_CB,),
                in_specs=[some_channels(GRAD_CB)] * 2
                + [chunk_spec] * ns
                + xi_spec
                + tables(yi, zi, zf, yf)
                + xf_spec,
                out_specs=[some_channels(GRAD_CB)] + [chunk_spec] * ns,
                scratch_shapes=[b_scr, r_scr],
            ),
            out_shape=[big] + [chunk] * ns,
            compiler_params=params(),
            cost_estimate=cost(cells * 1024, cells * 6),
            name="gelu_gradient",
        )(me_arr, pre, cotangent, *chunks, *xi_pre, yi, zi, zf, yf, *xf)

    def pair_call(field, dpre):
        return pl.pallas_call(
            pair_kernel,
            grid=(rows // 2,),
            in_specs=[two_rows, two_rows],
            out_specs=whole((channels, channels)),
            out_shape=jax.ShapeDtypeStruct((channels, channels), f32),
            scratch_shapes=[pltpu.VMEM((size, size), f32)],
            compiler_params=params(),
            cost_estimate=cost(cells * 512, cells * 4),
            name="point_gradient",
        )(field, dpre)

    def back_call(me_arr, dpre, point_weight, chunks):
        return pl.pallas_call(
            functools.partial(back_kernel, ns),
            grid_spec=pltpu.PrefetchScalarGridSpec(
                num_scalar_prefetch=1,
                grid=(rows // 2,),
                in_specs=[two_rows]
                + tables(point_weight)
                + [chunk_spec] * ns
                + xi_spec
                + tables(yi, zi),
                out_specs=two_rows,
                scratch_shapes=[b_scr, pltpu.VMEM((channels, NY, GROUP * 2 * MZ), bf16), kron_scr],
            ),
            out_shape=big,
            compiler_params=params(),
            cost_estimate=cost(cells * 1024, cells * 4),
            name="field_gradient",
        )(me_arr, dpre, point_weight, *chunks, *xi_back, yi, zi)

    modes = MX * MZ
    w_block = pl.BlockSpec((1, MX, MZ, channels, channels), lambda p, k: (p, 0, k, 0, 0))

    def weight_call(spec_weight):
        return pl.pallas_call(
            weight_kernel,
            grid=(2, own_ky),
            in_specs=[w_block],
            out_specs=pl.BlockSpec(
                (1, channels, 1, channels, modes), lambda p, k: (p, 0, k, 0, 0)
            ),
            out_shape=jax.ShapeDtypeStruct((2, channels, own_ky, channels, modes), bf16),
            scratch_shapes=[pltpu.VMEM((modes * channels, LANES), f32)],
            compiler_params=params(axes=2),
            cost_estimate=cost(0, 2 * own_ky * modes * channels * LANES * 2),
            name="weight_layout",
        )(spec_weight)

    def spec_call(us, gs):
        one_ky = pl.BlockSpec((1, channels, width), lambda k: (k, 0, 0))
        return pl.pallas_call(
            functools.partial(outer_kernel, len(us)),
            grid=(own_ky,),
            in_specs=[one_ky] * (2 * len(us)),
            out_specs=pl.BlockSpec((2, MX, MZ, channels, channels), lambda k: (0, 0, k, 0, 0)),
            out_shape=jax.ShapeDtypeStruct((2, MX, own_ky * MZ, channels, channels), f32),
            scratch_shapes=[pltpu.VMEM((2, modes * channels, LANES), f32)],
            compiler_params=params(),
            cost_estimate=cost(0, 2 * own_ky * modes * channels * LANES * 4),
            name="weight_gradient",
        )(*us, *gs)

    return {
        "field": field_call,
        "point": point_call,
        "mix": mix_call,
        "grad": grad_call,
        "pair": pair_call,
        "back": back_call,
        "weights": weight_call,
        "spec": spec_call,
    }


def fast_device(ns, nchan, field, cotangent, spec_weight, point_weight, bias):
    channels = field.shape[1]
    me = lax.axis_index("slab")
    me_arr = me[None].astype(jnp.int32)
    calls = make_calls(ns, field.shape)

    def swap(chunks, axis, size):
        got = [chunks[0]]
        for k in range(1, size):
            pairs = [(i, (i + k) % size) for i in range(size)]
            got.append(lax.ppermute(chunks[k], axis, pairs))
        return got

    field_chunks = calls["field"](me_arr, field)
    w = calls["weights"](spec_weight)
    pre = calls["point"](field, point_weight, bias)
    uhat, vhat = calls["mix"](False, swap(field_chunks, "slab", ns), w)
    vhats = swap([vhat] * ns, "slab", ns)
    dpre, *grad_chunks = calls["grad"](me_arr, pre, cotangent, vhats)
    u_all = swap([uhat] * nchan, "chan", nchan)

    point_part = calls["pair"](field, dpre)
    ghat, hhat = calls["mix"](True, swap(grad_chunks, "slab", ns), w)
    hhats = swap([hhat] * ns, "slab", ns)
    g_all = swap([ghat] * nchan, "chan", nchan)
    field_grad = calls["back"](me_arr, dpre, point_weight, hhats)

    spec_grad = calls["spec"](u_all, g_all)

    norm_scale = 1.0 / math.sqrt(nchan * NX * NY * NZ)
    dc = jnp.where(me == 0, ghat[0, :, 0], 0.0) * (1.0 / SCALE_FORWARD)
    tail = jnp.concatenate([point_part, dc[None, :]], axis=0)
    for axis, count in (("chan", nchan), ("slab", ns)):
        tail = sum(swap([tail] * count, axis, count))
    tail = tail * norm_scale
    return field_grad, spec_grad, tail[:channels], tail[channels]


def plain_device(field, cotangent, spec_weight, point_weight, bias):
    samples, channels, rows, _, _ = field.shape
    high = lax.Precision.HIGHEST

    def con(form, a, b):
        return jnp.einsum(form, a, b, precision=high)

    yc, ys = (jnp.asarray(t) for t in mode_table(NY, MY, True))
    zc, zs = (jnp.asarray(t) for t in mode_table(NZ, MZ, False))
    xc, xs = (jnp.asarray(t) for t in mode_table(NX, MX, True))
    y_table = jnp.concatenate([yc, ys], axis=1).astype(bf16)
    z_table = jnp.concatenate([zc, zs], axis=1)
    pairs = MY * MZ

    def to_spectrum(values):
        q = jnp.einsum("scxyz,yk->scxkz", values, y_table, preferred_element_type=f32)
        zr = con("scxkz,zj->scxkj", q[:, :, :, :MY], z_table)
        zm = con("scxkz,zj->scxkj", q[:, :, :, MY:], z_table)
        real = zr[..., :MZ] - zm[..., MZ:]
        imag = zr[..., MZ:] + zm[..., :MZ]
        local = jnp.stack([real, imag]).reshape(2, samples, channels, rows, pairs)
        a, b = lax.all_to_all(local, "slab", split_axis=4, concat_axis=3, tiled=True)
        real = con("scxk,xm->scmk", a, xc) - con("scxk,xm->scmk", b, xs)
        imag = con("scxk,xm->scmk", b, xc) + con("scxk,xm->scmk", a, xs)
        return real * SCALE_FORWARD, imag * SCALE_FORWARD

    def from_spectrum(a, b):
        real = con("scmk,xm->scxk", a, xc) + con("scmk,xm->scxk", b, xs)
        imag = con("scmk,xm->scxk", b, xc) - con("scmk,xm->scxk", a, xs)
        both = jnp.stack([real, imag])
        both = lax.all_to_all(both, "slab", split_axis=3, concat_axis=4, tiled=True)
        real, imag = both.reshape(2, samples, channels, rows, MY, MZ)
        fr = con("scxkj,zj->scxkz", real, zc) + con("scxkj,zj->scxkz", imag, zs)
        fi = con("scxkj,zj->scxkz", imag, zc) - con("scxkj,zj->scxkz", real, zs)
        f = jnp.concatenate([fr, fi], axis=3).astype(bf16)
        out = jnp.einsum("scxkz,yk->scxyz", f, y_table, preferred_element_type=f32)
        return out * SCALE_INVERSE

    wr, wi = spec_weight.astype(f32)
    ur, ui = to_spectrum(field)
    mix = functools.partial(con, "scmk,mkco->somk")
    spectral = from_spectrum(mix(ur, wr) - mix(ui, wi), mix(ui, wr) + mix(ur, wi))
    point = jnp.einsum("co,scxyz->soxyz", point_weight, field, preferred_element_type=f32)
    pre = (spectral + point + bias[None, :, None, None, None]) * GK
    dpre = (cotangent.astype(f32) * gelu_slope(pre)).astype(bf16)
    gr, gi = to_spectrum(dpre)
    mix = functools.partial(con, "somk,mkco->scmk")
    back = from_spectrum(mix(gr, wr) + mix(gi, wi), mix(gi, wr) - mix(gr, wi))
    point = jnp.einsum("co,soxyz->scxyz", point_weight, dpre, preferred_element_type=f32)
    field_grad = (back + point).astype(bf16)
    outer = functools.partial(con, "scmk,somk->mkco")
    dw = jnp.stack([outer(ur, gr) + outer(ui, gi), outer(ur, gi) - outer(ui, gr)])
    spec_grad = lax.psum(dw, "chan")
    point_part = jnp.einsum("scxyz,soxyz->co", field, dpre, preferred_element_type=f32)
    bias_part = jnp.sum(dpre.astype(f32), axis=(0, 2, 3, 4))
    point_part, bias_part = lax.psum((point_part, bias_part), ("slab", "chan"))
    scale = 1.0 / math.sqrt(samples * lax.axis_size("chan") * NX * NY * NZ)
    return field_grad, spec_grad, point_part * scale, bias_part * scale


def solution(mesh):
    ns, nchan = mesh.shape["slab"], mesh.shape["chan"]

    def per_device(field, *rest):
        samples, _, rows, _, _ = field.shape
        if MY % ns == 0 and rows % (2 * GROUP) == 0 and samples == 1:
            return fast_device(ns, nchan, field, *rest)
        return plain_device(field, *rest)

    return jax.shard_map(
        per_device,
        mesh=mesh,
        in_specs=(
            P(("groups", "chan"), None, "slab", None, None),
            P(("groups", "chan"), None, "slab", None, None),
            P(None, None, "slab", None, None),
            P(),
            P(),
        ),
        out_specs=(
            P(("groups", "chan"), None, "slab", None, None),
            P("groups", None, "slab", None, None),
            P("groups", None),
            P("groups"),
        ),
        check_vma=False,
    )
```

```python
import functools
import math

import jax
import jax.numpy as jnp
import numpy as np
from jax import lax
from jax.experimental import pallas as pl
from jax.experimental.pallas import tpu as pltpu
from jax.sharding import PartitionSpec as P

NX = 128
NY = 128
NZ = 128
MX = 16
MY = 16
MZ = 8
LANES = 128
GROUP = 8

FIELD_CB = 4
PAD = 8
ROWS = 4
GRAD_CB = 4

f32 = jnp.float32
bf16 = jnp.bfloat16

GA = 0.7978845608
GB = 0.044715
GK = (GA * GB) ** (1.0 / 3.0)
GALPHA = GA / GK
SLOPE = 1.5

SCALE_FORWARD = 1.0 / math.sqrt(NX * NY * NZ)
SCALE_INVERSE = 1.0 / math.sqrt(MX * MY * MZ)


def mode_table(length, count, signed):
    position = np.arange(length)[:, None]
    index = np.arange(count)[None, :]
    frequency = np.where(index >= count // 2, index - count, index) if signed else index
    angle = (position * frequency % length).astype(np.float64) * (2.0 * math.pi / length)
    return np.cos(angle).astype(np.float32), (-np.sin(angle)).astype(np.float32)


def bf(value):
    return np.asarray(value, np.float32).astype(jnp.bfloat16)


def split_bf(value):
    high = bf(value)
    return high, bf(np.asarray(value, np.float32) - high.astype(np.float32))


def z_forward_table():
    zc, zs = mode_table(NZ, MZ, False)
    block = np.concatenate([zc, zs], axis=1)
    table = np.zeros((GROUP, NZ, GROUP, 2 * MZ), np.float32)
    for x in range(GROUP):
        table[x, :, x] = block
    return bf(table.reshape(GROUP * NZ, GROUP * 2 * MZ))


def z_inverse_table():
    zc, zs = mode_table(NZ, MZ, False)
    block = np.concatenate([zc, zs], axis=1).T
    table = np.zeros((GROUP // 2, GROUP, 2 * MZ, 2, NZ), np.float32)
    for x in range(GROUP):
        table[x // 2, x, :, x % 2] = block
    return bf(table.reshape(GROUP // 2, GROUP * 2 * MZ, 2 * NZ))


def y_tables():
    yc, ys = mode_table(NY, MY, True)
    forward = np.concatenate([yc.T, ys.T], axis=0)
    inverse = np.concatenate([yc, ys, yc, ys], axis=1)
    return bf(forward), bf(inverse)


def x_forward_table(scale):
    xc, xs = mode_table(NX, MX, True)
    table = np.zeros((NX, 2, MZ, 2, MX, MZ), np.float32)
    for kz in range(MZ):
        table[:, 0, kz, 0, :, kz] = xc
        table[:, 1, kz, 0, :, kz] = -xs
        table[:, 0, kz, 1, :, kz] = xs
        table[:, 1, kz, 1, :, kz] = xc
    return table.reshape(NX * 2 * MZ, 2 * MX * MZ) * (scale * SCALE_FORWARD)


def x_inverse_table(scale, ns):
    xc, xs = mode_table(NX, MX, True)
    table = np.zeros((2, MX, MZ, 2, NX, 2, MZ), np.float32)
    for kz in range(MZ):
        re_re, im_re = xc.T, xs.T
        re_im, im_im = -xs.T, xc.T
        table[0, :, kz, 0, :, 0, kz] = re_re
        table[1, :, kz, 0, :, 0, kz] = im_re
        table[0, :, kz, 0, :, 1, kz] = re_im
        table[1, :, kz, 0, :, 1, kz] = im_im
        table[0, :, kz, 1, :, 0, kz] = re_im
        table[1, :, kz, 1, :, 0, kz] = im_im
        table[0, :, kz, 1, :, 1, kz] = -re_re
        table[1, :, kz, 1, :, 1, kz] = -im_re
    table = table.reshape(2 * MX * MZ, 2, ns, NX // ns * 2 * MZ).transpose(2, 0, 1, 3)
    return table.reshape(ns, 2 * MX * MZ, -1) * scale


def dot(a, b):
    return jnp.dot(a, b, preferred_element_type=f32)


def parts(value):
    high = value.astype(bf16)
    return high, (value - high.astype(f32)).astype(bf16)


def dot3(a, bh, bl):
    ah, al = parts(a)
    return dot(ah, bh) + dot(al, bh) + dot(ah, bl)


def z_forward(tiles, zf):
    wide = jnp.concatenate(
        [
            jnp.concatenate(tiles[g : g + GROUP], axis=1)
            for g in range(0, len(tiles), GROUP)
        ],
        axis=0,
    )
    q = dot(wide, zf).astype(bf16)
    return [q[g : g + NY] for g in range(0, q.shape[0], NY)]


def y_forward(groups, yf):
    r = dot(yf, jnp.concatenate(groups, axis=1))
    top, bot = r[:MY], r[MY:]
    lanes = bot.shape[1]
    at = lax.broadcasted_iota(jnp.int32, top.shape, 1) % (2 * MZ)
    return jnp.where(
        at < MZ, top - pltpu.roll(bot, lanes - MZ, 1), top + pltpu.roll(bot, MZ, 1)
    )


def x_forward_out(me, ns, channels, r_scr, xfh, xfl, outs):
    rows = (MY // ns) * channels
    r = jnp.concatenate([r_scr[i] for i in range(r_scr.shape[0])], axis=1)
    width = xfh.shape[1]
    done = dot3(r, xfh[...], xfl[...])
    for i in range(width // LANES):
        r_scr[i] = done[:, i * LANES : (i + 1) * LANES]
    for k in range(ns):
        owner = lax.rem(me + k, ns)
        at = pl.ds(pl.multiple_of(owner * rows, rows), rows)
        for i in range(width // LANES):
            outs[k][:, :, i * LANES : (i + 1) * LANES] = r_scr[i, at, :].reshape(
                MY // ns, channels, LANES
            )


def x_inverse_in(me, ns, channels, ins, xih, xil, b_scr):
    rows = (MY // ns) * channels
    for k in range(ns):
        owner = lax.rem(me + ns - k, ns)
        h = ins[k][...].reshape(rows, -1)
        b = dot3(h, xih[0], xil[0])
        for i in range(b_scr.shape[0]):
            at = pl.ds(pl.multiple_of(owner * rows, rows), rows)
            b_scr[i, at, :] = b[:, i * LANES : (i + 1) * LANES]


def put_channel(scr, c, channels, value):
    for i in range(scr.shape[0]):
        scr[i, pl.ds(c, MY, stride=channels), :] = value[:, i * LANES : (i + 1) * LANES]


def get_channel(scr, c, channels, blocks):
    return jnp.concatenate(
        [scr[i, pl.ds(c, MY, stride=channels), :] for i in blocks], axis=1
    )


def y_inverse(bs, yi):
    lanes = bs[0].shape[1] // 2
    rhs = []
    for b in bs:
        high, low = parts(b)
        rhs.append(
            jnp.concatenate(
                [high[:, :lanes], high[:, lanes:], low[:, :lanes], low[:, lanes:]], axis=0
            )
        )
    return dot(yi, jnp.concatenate(rhs, axis=1)).astype(bf16)


def kron_halves(block):
    channels, _, lanes = block.shape
    wide = block.astype(f32).reshape(channels, 2, 8, lanes)
    return [wide[:, h].reshape(channels * 8, lanes).astype(bf16) for h in range(2)]


def row_pair(ref, x, y):
    return jnp.concatenate([ref[0, :, x + i, y : y + 16, :] for i in range(2)], axis=2)


def whole_rows(value, at, lanes):
    size = value.shape[0] // 8
    two = [value[:, a : a + lanes].reshape(size, 8, lanes) for a in (at, at + lanes)]
    return jnp.concatenate(two, axis=1)


def put_rows(ref, x, y, value):
    value = value.astype(bf16)
    ref[0, :, x, y : y + 16, :] = value[:, :, :NZ]
    ref[0, :, x + 1, y : y + 16, :] = value[:, :, NZ:]


def pick_rows(channels):
    row = lax.broadcasted_iota(jnp.int32, (channels * 8, channels), 0)
    col = lax.broadcasted_iota(jnp.int32, (channels * 8, channels), 1)
    return row // 8 == col


def same_cell(channels):
    size = channels * 8
    row = lax.broadcasted_iota(jnp.int32, (size, size), 0)
    col = lax.broadcasted_iota(jnp.int32, (size, size), 1)
    return row % 8 == col % 8


def kron_rows(point, turned):
    channels = point.shape[0]
    pick = jnp.where(pick_rows(channels), 1.0, 0.0).astype(bf16)
    nt = (((1,), (1,)), ((), ()))
    tn = (((1,), (0,)), ((), ()))
    left = lax.dot_general(pick, point, nt if turned else tn, preferred_element_type=f32)
    full = lax.dot_general(left.astype(bf16), pick, nt, preferred_element_type=f32)
    return jnp.where(same_cell(channels), full, 0.0).astype(bf16)


def field_kernel(ns, channels, me_ref, field, zf, yf, xfh, xfl, *rest):
    outs, r_scr = rest[:ns], rest[ns]
    step = pl.program_id(0)
    rows = field.shape[2]
    lanes = rows * 2 * MZ
    groups = []
    for i in range(FIELD_CB):
        groups += z_forward([field[0, i, x] for x in range(rows)], zf[...])
    spectra = y_forward(groups, yf[...])
    for i in range(FIELD_CB):
        put_channel(r_scr, step * FIELD_CB + i, channels, spectra[:, i * lanes : (i + 1) * lanes])

    @pl.when(step == pl.num_programs(0) - 1)
    def _():
        x_forward_out(me_ref[0], ns, channels, r_scr, xfh, xfl, outs)


def point_kernel(field, point, bias, out, kron):
    channels = field.shape[1]

    @pl.when(pl.program_id(0) == 0)
    def _():
        kron[...] = kron_rows(point[...], True)

    bias_rows = jnp.sum(jnp.where(pick_rows(channels), bias[...], 0.0), axis=1, keepdims=True) * GK
    bias_16 = jnp.concatenate([bias_rows.reshape(channels, 8, 1)] * 2, axis=1)

    for x in range(0, field.shape[2], 2):
        halves = []
        for y in range(0, NY, 16):
            halves += kron_halves(row_pair(field, x, y))
        lanes = halves[0].shape[1]
        done = dot(kron[...], jnp.concatenate(halves, axis=1))
        for y in range(0, NY, 16):
            put_rows(out, x, y, whole_rows(done, y // 8 * lanes, lanes) * GK + bias_16)


def gelu_slope(v):
    n = v * v
    t = jnp.tanh(v * (n + GALPHA))
    return (1.0 + t) * (0.5 / SLOPE + (1.0 - t) * (v * (n + GALPHA / 3.0)))


def grad_kernel(ns, channels, me_ref, pre, cot, *rest):
    ins = rest[:ns]
    xih, xil, yi, zi, zf, yf, xfh, xfl = rest[ns : ns + 8]
    dpre = rest[ns + 8]
    outs = rest[ns + 9 : ns + 9 + ns]
    b_scr, r_scr = rest[ns + 9 + ns :]
    step = pl.program_id(0)
    rows = pre.shape[2]
    width = GROUP * 2 * MZ
    groups = rows // GROUP

    @pl.when(step == 0)
    def _():
        x_inverse_in(me_ref[0], ns, channels, ins, xih, xil, b_scr)

    lanes = rows * 2 * MZ
    blocks = range(b_scr.shape[0])
    wide = y_inverse(
        [get_channel(b_scr, step * GRAD_CB + i, channels, blocks) for i in range(GRAD_CB)], yi[...]
    )
    pairs = GROUP // 2

    def inverse(i, j):
        first = i * groups * width
        rows_of = [wide[:, first + g * width : first + (g + 1) * width] for g in range(groups)]
        return dot(jnp.concatenate(rows_of, axis=0), zi[j])

    def slope(i, j, v_all):
        for g in range(groups):
            x = g * GROUP + 2 * j
            v = v_all[g * NY : (g + 1) * NY]
            v = v + jnp.concatenate([pre[0, i, x], pre[0, i, x + 1]], axis=1).astype(f32)
            w = jnp.concatenate([cot[0, i, x], cot[0, i, x + 1]], axis=1)
            d = (w.astype(f32) * gelu_slope(v)).astype(bf16)
            dpre[0, i, x] = d[:, :NZ]
            dpre[0, i, x + 1] = d[:, NZ:]

    done = []
    for i in range(GRAD_CB + 1):
        for j in range(pairs):
            if i < GRAD_CB:
                slope(i, j, inverse(i, j))
            if i and j == 0:
                done += z_forward([dpre[0, i - 1, x] for x in range(rows)], zf[...])
    spectra = y_forward(done, yf[...])
    for i in range(GRAD_CB):
        put_channel(r_scr, step * GRAD_CB + i, channels, spectra[:, i * lanes : (i + 1) * lanes])

    @pl.when(step == pl.num_programs(0) - 1)
    def _():
        x_forward_out(me_ref[0], ns, channels, r_scr, xfh, xfl, outs)


def pair_kernel(field, dpre, out, acc):
    channels = field.shape[1]
    step = pl.program_id(0)

    @pl.when(step == 0)
    def _():
        acc[...] = jnp.zeros_like(acc)

    for x in range(0, field.shape[2], 2):
        lefts, rights = [], []
        for y in range(0, NY, 16):
            lefts += kron_halves(row_pair(field, x, y))
            rights += kron_halves(row_pair(dpre, x, y))
        acc[...] += lax.dot_general(
            jnp.concatenate(lefts, axis=1),
            jnp.concatenate(rights, axis=1),
            (((1,), (1,)), ((), ())),
            preferred_element_type=f32,
        )

    @pl.when(step == pl.num_programs(0) - 1)
    def _():
        same = jnp.where(same_cell(channels), acc[...], 0.0)
        pick = jnp.where(pick_rows(channels), 1.0, 0.0)
        high = lax.Precision.HIGHEST
        left = jnp.dot(same, pick, precision=high, preferred_element_type=f32)
        out[...] = lax.dot_general(
            pick, left, (((0,), (0,)), ((), ())), precision=high, preferred_element_type=f32
        ) * SLOPE


def back_kernel(ns, me_ref, dpre, point, *rest):
    ins = rest[:ns]
    xih, xil, yi, zi = rest[ns : ns + 4]
    out, b_scr, g_scr, kron = rest[ns + 4 :]
    channels = dpre.shape[1]
    step = pl.program_id(0)
    width = GROUP * 2 * MZ

    @pl.when(step == 0)
    def _():
        x_inverse_in(me_ref[0], ns, channels, ins, xih, xil, b_scr)
        kron[...] = kron_rows(point[...], False)

    per_group = GROUP // dpre.shape[2]

    @pl.when(step % per_group == 0)
    def _():
        group = step // per_group
        turned = group + b_scr.shape[0] // 2
        wide = y_inverse(
            [get_channel(b_scr, c, channels, (group, turned)) for c in range(channels)], yi[...]
        )
        for c in range(channels):
            g_scr[c] = wide[:, c * width : (c + 1) * width]

    flat = g_scr[...].reshape(channels * NY, width)
    pairs = dpre.shape[2] // 2
    for p in range(pairs):
        x = 2 * p
        halves = []
        for y in range(0, NY, 16):
            halves += kron_halves(row_pair(dpre, x, y))
        lanes = halves[0].shape[1]
        point = dot(kron[...], jnp.concatenate(halves, axis=1))
        spec = dot(flat, zi[step % per_group * pairs + p]).reshape(channels, NY, lanes)
        for y in range(0, NY, 16):
            one = whole_rows(point, y // 8 * lanes, lanes) * SLOPE
            put_rows(out, x, y, one + spec[:, y : y + 16])


def mix_kernel(ns, adjoint, *refs):
    ins, weights, total, out = refs[:ns], refs[ns], refs[ns + 1], refs[ns + 2]
    rows, channels, width = total.shape
    half = width // 2
    u = ins[0][...]
    for k in range(1, ns):
        u = u + ins[k][...]
    total[...] = u
    for ky in range(rows):
        if not adjoint:
            real = jnp.zeros((channels, half), f32)
            imag = jnp.zeros((channels, half), f32)
            for c in range(channels):
                a, b = total[ky, pl.ds(c, 1), :half], total[ky, pl.ds(c, 1), half:]
                wr, wi = weights[0, c, ky].astype(f32), weights[1, c, ky].astype(f32)
                real = real + (wr * a - wi * b)
                imag = imag + (wr * b + wi * a)
            out[ky, :, :half] = real
            out[ky, :, half:] = imag
        else:
            a, b = total[ky, :, :half], total[ky, :, half:]
            for c in range(channels):
                wr, wi = weights[0, c, ky].astype(f32), weights[1, c, ky].astype(f32)
                out[ky, pl.ds(c, 1), :half] = jnp.sum(wr * a + wi * b, axis=0, keepdims=True)
                out[ky, pl.ds(c, 1), half:] = jnp.sum(wr * b - wi * a, axis=0, keepdims=True)


def weight_kernel(weights, out, scr):
    _, kxs, kzs, channels, _ = weights.shape
    modes = kxs * kzs
    stride = channels + PAD
    wide = weights[...].astype(f32).reshape(modes, channels, channels)
    scr[:, :channels, :channels] = wide
    flat = scr.reshape(modes * stride, LANES)
    per = LANES // channels
    lane = lax.broadcasted_iota(jnp.int32, (modes, LANES), 1) // channels
    for c in range(0, channels, per):
        packed = flat[pl.ds(c, modes, stride=stride), :]
        for q in range(1, per):
            more = flat[pl.ds(c + q, modes, stride=stride), :]
            packed = jnp.where(lane == q, pltpu.roll(more, q * channels, 1), packed)
        turned = packed.T.astype(bf16)
        for q in range(per):
            out[0, c + q, 0] = turned[q * channels : (q + 1) * channels]


def outer_kernel(samples, *refs):
    us, gs, out, scr = refs[:samples], refs[samples : 2 * samples], refs[-2], refs[-1]
    channels = us[0].shape[1]
    modes = us[0].shape[2] // 2
    per = LANES // channels
    tn = (((0,), (0,)), ((), ()))

    def stack(refs):
        wide = jnp.concatenate([ref[0] for ref in refs], axis=1)
        return jnp.concatenate(parts(wide), axis=0)

    def table(lanes, of):
        row = lax.broadcasted_iota(jnp.int32, (2 * channels, lanes), 0) % channels
        col = lax.broadcasted_iota(jnp.int32, (2 * channels, lanes), 1)
        return jnp.where(row == of(col), 1.0, 0.0).astype(bf16)

    stride = channels + PAD
    flat = scr.reshape(2, modes * stride, LANES)
    by_o = table(LANES, lambda col: col % channels)
    by_c = table(channels * channels, lambda col: col // channels)
    g_all = lax.dot_general(stack(gs), by_o, tn, preferred_element_type=f32)
    u_all = lax.dot_general(stack(us), by_c, tn, preferred_element_type=f32)
    for n in range(channels // per):
        real = imag = None
        for s in range(samples):
            at = 2 * s * modes
            gr, gi = g_all[at : at + modes], g_all[at + modes : at + 2 * modes]
            u = u_all[at : at + 2 * modes, n * LANES : (n + 1) * LANES]
            ur, ui = u[:modes], u[modes:]
            re, im = ur * gr + ui * gi, ur * gi - ui * gr
            real = re if real is None else real + re
            imag = im if imag is None else imag + im
        for p, value in enumerate((real, imag)):
            for q in range(per):
                one = value if q == 0 else pltpu.roll(value, LANES - q * channels, 1)
                flat[p, pl.ds(n * per + q, modes, stride=stride), :] = one
    out[...] = scr[:, :, :channels, :channels].reshape(out.shape)


def whole(shape):
    return pl.BlockSpec(shape, lambda *_: (0,) * len(shape))


def params(mib=60, axes=1):
    return pltpu.CompilerParams(
        dimension_semantics=("arbitrary",) * axes, vmem_limit_bytes=mib * 2**20
    )


def make_calls(ns, shape):
    _, channels, rows, _, _ = shape
    own_ky = MY // ns
    width = 2 * MX * MZ
    lanes = rows * 2 * MZ
    size = channels * 8

    zf = jnp.asarray(z_forward_table())
    zi = jnp.asarray(z_inverse_table())
    yf, yi = (jnp.asarray(t) for t in y_tables())
    xf = [jnp.asarray(t) for t in split_bf(x_forward_table(1.0))]
    xf_grad = [jnp.asarray(t) for t in split_bf(x_forward_table(SLOPE))]
    xf_spec = [pl.BlockSpec((lanes, width), lambda i, at: (at[0], 0))] * 2
    xi_pre = [jnp.asarray(t) for t in split_bf(x_inverse_table(SCALE_INVERSE * GK, ns))]
    xi_back = [jnp.asarray(t) for t in split_bf(x_inverse_table(SCALE_INVERSE, ns))]
    xi_spec = [pl.BlockSpec((1, width, 2 * lanes), lambda i, at: (at[0], 0, 0))] * 2

    chunk = jax.ShapeDtypeStruct((own_ky, channels, width), f32)
    chunk_spec = whole(chunk.shape)

    def some_channels(count):
        return pl.BlockSpec((1, count, rows, NY, NZ), lambda c, *_: (0, c, 0, 0, 0))

    some_rows = pl.BlockSpec((1, channels, ROWS, NY, NZ), lambda x, *_: (0, 0, x, 0, 0))
    big = jax.ShapeDtypeStruct(shape, bf16)
    cells = channels * rows * NY * NZ
    r_scr = pltpu.VMEM((lanes // LANES, MY * channels, LANES), f32)
    b_scr = pltpu.VMEM((2 * lanes // LANES, MY * channels, LANES), f32)
    kron_scr = pltpu.VMEM((size, size), bf16)

    def cost(flops, moved):
        return pl.CostEstimate(flops=int(flops), bytes_accessed=int(moved), transcendentals=0)

    def tables(*arrays):
        return [whole(a.shape) for a in arrays]

    def field_call(me_arr, field):
        return pl.pallas_call(
            functools.partial(field_kernel, ns, channels),
            grid_spec=pltpu.PrefetchScalarGridSpec(
                num_scalar_prefetch=1,
                grid=(channels // FIELD_CB,),
                in_specs=[some_channels(FIELD_CB)] + tables(zf, yf) + xf_spec,
                out_specs=[chunk_spec] * ns,
                scratch_shapes=[r_scr],
            ),
            out_shape=[chunk] * ns,
            compiler_params=params(),
            cost_estimate=cost(cells * 512, cells * 2),
            name="field_spectrum",
        )(me_arr, field, zf, yf, *xf)

    def point_call(field, point_weight, bias):
        return pl.pallas_call(
            point_kernel,
            grid=(rows // ROWS,),
            in_specs=[some_rows] + tables(point_weight, bias[None]),
            out_specs=some_rows,
            out_shape=big,
            scratch_shapes=[kron_scr],
            compiler_params=params(),
            cost_estimate=cost(cells * 512, cells * 4),
            name="pointwise",
        )(field, point_weight, bias[None])

    def mix_call(adjoint, chunks, w):
        return pl.pallas_call(
            functools.partial(mix_kernel, ns, adjoint),
            grid=(1,),
            in_specs=[chunk_spec] * ns + tables(w),
            out_specs=[chunk_spec, chunk_spec],
            out_shape=[chunk, chunk],
            compiler_params=params(),
            name="mix_adjoint" if adjoint else "mix",
        )(*chunks, w)

    def grad_call(me_arr, pre, cotangent, chunks):
        return pl.pallas_call(
            functools.partial(grad_kernel, ns, channels),
            grid_spec=pltpu.PrefetchScalarGridSpec(
                num_scalar_prefetch=1,
                grid=(channels // GRAD_CB,),
                in_specs=[some_channels(GRAD_CB)] * 2
                + [chunk_spec] * ns
                + xi_spec
                + tables(yi, zi, zf, yf)
                + xf_spec,
                out_specs=[some_channels(GRAD_CB)] + [chunk_spec] * ns,
                scratch_shapes=[b_scr, r_scr],
            ),
            out_shape=[big] + [chunk] * ns,
            compiler_params=params(),
            cost_estimate=cost(cells * 1024, cells * 6),
            name="gelu_gradient",
        )(me_arr, pre, cotangent, *chunks, *xi_pre, yi, zi, zf, yf, *xf_grad)

    def pair_call(field, dpre, part=0, count=1):
        steps = rows // ROWS // count
        part_rows = pl.BlockSpec(
            (1, channels, ROWS, NY, NZ), lambda x: (0, 0, x + part * steps, 0, 0)
        )
        return pl.pallas_call(
            pair_kernel,
            grid=(steps,),
            in_specs=[part_rows, part_rows],
            out_specs=whole((channels, channels)),
            out_shape=jax.ShapeDtypeStruct((channels, channels), f32),
            scratch_shapes=[pltpu.VMEM((size, size), f32)],
            compiler_params=params(),
            cost_estimate=cost(cells * 512 // count, cells * 4 // count),
            name="point_gradient",
        )(field, dpre)

    def back_call(me_arr, dpre, point_weight, chunks):
        return pl.pallas_call(
            functools.partial(back_kernel, ns),
            grid_spec=pltpu.PrefetchScalarGridSpec(
                num_scalar_prefetch=1,
                grid=(rows // ROWS,),
                in_specs=[some_rows]
                + tables(point_weight)
                + [chunk_spec] * ns
                + xi_spec
                + tables(yi, zi),
                out_specs=some_rows,
                scratch_shapes=[b_scr, pltpu.VMEM((channels, NY, GROUP * 2 * MZ), bf16), kron_scr],
            ),
            out_shape=big,
            compiler_params=params(),
            cost_estimate=cost(cells * 1024, cells * 4),
            name="field_gradient",
        )(me_arr, dpre, point_weight, *chunks, *xi_back, yi, zi)

    modes = MX * MZ
    w_block = pl.BlockSpec((1, MX, MZ, channels, channels), lambda p, k: (p, 0, k, 0, 0))

    def weight_call(spec_weight):
        return pl.pallas_call(
            weight_kernel,
            grid=(2, own_ky),
            in_specs=[w_block],
            out_specs=pl.BlockSpec(
                (1, channels, 1, channels, modes), lambda p, k: (p, 0, k, 0, 0)
            ),
            out_shape=jax.ShapeDtypeStruct((2, channels, own_ky, channels, modes), bf16),
            scratch_shapes=[pltpu.VMEM((modes, channels + PAD, LANES), f32)],
            compiler_params=params(axes=2),
            cost_estimate=cost(0, 2 * own_ky * modes * channels * LANES * 2),
            name="weight_layout",
        )(spec_weight)

    def spec_call(every):
        one_u = pl.BlockSpec((1, channels, width), lambda k: (k, 0, 0))
        one_g = pl.BlockSpec((1, channels, width), lambda k: (own_ky + k, 0, 0))
        return pl.pallas_call(
            functools.partial(outer_kernel, len(every)),
            grid=(own_ky,),
            in_specs=[one_u] * len(every) + [one_g] * len(every),
            out_specs=pl.BlockSpec((2, MX, MZ, channels, channels), lambda k: (0, 0, k, 0, 0)),
            out_shape=jax.ShapeDtypeStruct((2, MX, own_ky * MZ, channels, channels), f32),
            scratch_shapes=[pltpu.VMEM((2, modes, channels + PAD, LANES), f32)],
            compiler_params=params(),
            cost_estimate=cost(0, 2 * own_ky * modes * channels * LANES * 4),
            name="weight_gradient",
        )(*every, *every)

    return {
        "field": field_call,
        "point": point_call,
        "mix": mix_call,
        "grad": grad_call,
        "pair": pair_call,
        "back": back_call,
        "weights": weight_call,
        "spec": spec_call,
    }


def fast_device(ns, nchan, field, cotangent, spec_weight, point_weight, bias):
    channels = field.shape[1]
    me = lax.axis_index("slab")
    me_arr = me[None].astype(jnp.int32)
    calls = make_calls(ns, field.shape)

    def swap(chunks, axis, size):
        got = [chunks[0]]
        for k in range(1, size):
            pairs = [(i, (i + k) % size) for i in range(size)]
            got.append(lax.ppermute(chunks[k], axis, pairs))
        return got

    field_chunks = calls["field"](me_arr, field)
    w = calls["weights"](spec_weight)
    pre = calls["point"](field, point_weight, bias)
    uhat, vhat = calls["mix"](False, swap(field_chunks, "slab", ns), w)
    vhats = swap([vhat] * ns, "slab", ns)
    dpre, *grad_chunks = calls["grad"](me_arr, pre, cotangent, vhats)

    point_part = calls["pair"](field, dpre, 0, 2)
    ghat, hhat = calls["mix"](True, swap(grad_chunks, "slab", ns), w)
    hhats = swap([hhat] * ns, "slab", ns)
    dpre_later, _ = lax.optimization_barrier((dpre, hhat))
    point_part = point_part + calls["pair"](field, dpre_later, 1, 2)

    norm_scale = 1.0 / math.sqrt(nchan * NX * NY * NZ)
    dc = jnp.where(me == 0, ghat[0, :, 0], 0.0) * (1.0 / SCALE_FORWARD)
    tail = jnp.concatenate([point_part, dc[:, None]], axis=1)
    tail = jnp.pad(tail, ((0, 0), (0, ghat.shape[2] - tail.shape[1])))
    sample = jnp.concatenate([uhat, ghat, tail[None]], axis=0)
    every = swap([sample] * nchan, "chan", nchan)
    field_grad = calls["back"](me_arr, dpre, point_weight, hhats)
    every, field_grad = lax.optimization_barrier((every, field_grad))
    tails = swap([sum(one[-1, :, : channels + 1] for one in every)] * ns, "slab", ns)

    spec_grad = calls["spec"](every)
    tail = sum(tails) * norm_scale
    return field_grad, spec_grad, tail[:, :channels], tail[:, channels]


def plain_device(field, cotangent, spec_weight, point_weight, bias):
    samples, channels, rows, _, _ = field.shape
    high = lax.Precision.HIGHEST

    def con(form, a, b):
        return jnp.einsum(form, a, b, precision=high)

    yc, ys = (jnp.asarray(t) for t in mode_table(NY, MY, True))
    zc, zs = (jnp.asarray(t) for t in mode_table(NZ, MZ, False))
    xc, xs = (jnp.asarray(t) for t in mode_table(NX, MX, True))
    y_table = jnp.concatenate([yc, ys], axis=1).astype(bf16)
    z_table = jnp.concatenate([zc, zs], axis=1)
    pairs = MY * MZ

    def to_spectrum(values):
        q = jnp.einsum("scxyz,yk->scxkz", values, y_table, preferred_element_type=f32)
        zr = con("scxkz,zj->scxkj", q[:, :, :, :MY], z_table)
        zm = con("scxkz,zj->scxkj", q[:, :, :, MY:], z_table)
        real = zr[..., :MZ] - zm[..., MZ:]
        imag = zr[..., MZ:] + zm[..., :MZ]
        local = jnp.stack([real, imag]).reshape(2, samples, channels, rows, pairs)
        a, b = lax.all_to_all(local, "slab", split_axis=4, concat_axis=3, tiled=True)
        real = con("scxk,xm->scmk", a, xc) - con("scxk,xm->scmk", b, xs)
        imag = con("scxk,xm->scmk", b, xc) + con("scxk,xm->scmk", a, xs)
        return real * SCALE_FORWARD, imag * SCALE_FORWARD

    def from_spectrum(a, b):
        real = con("scmk,xm->scxk", a, xc) + con("scmk,xm->scxk", b, xs)
        imag = con("scmk,xm->scxk", b, xc) - con("scmk,xm->scxk", a, xs)
        both = jnp.stack([real, imag])
        both = lax.all_to_all(both, "slab", split_axis=3, concat_axis=4, tiled=True)
        real, imag = both.reshape(2, samples, channels, rows, MY, MZ)
        fr = con("scxkj,zj->scxkz", real, zc) + con("scxkj,zj->scxkz", imag, zs)
        fi = con("scxkj,zj->scxkz", imag, zc) - con("scxkj,zj->scxkz", real, zs)
        f = jnp.concatenate([fr, fi], axis=3).astype(bf16)
        out = jnp.einsum("scxkz,yk->scxyz", f, y_table, preferred_element_type=f32)
        return out * SCALE_INVERSE

    wr, wi = spec_weight.astype(f32)
    ur, ui = to_spectrum(field)
    mix = functools.partial(con, "scmk,mkco->somk")
    spectral = from_spectrum(mix(ur, wr) - mix(ui, wi), mix(ui, wr) + mix(ur, wi))
    point = jnp.einsum("co,scxyz->soxyz", point_weight, field, preferred_element_type=f32)
    pre = (spectral + point + bias[None, :, None, None, None]) * GK
    dpre = (cotangent.astype(f32) * gelu_slope(pre)).astype(bf16)
    gr, gi = to_spectrum(dpre)
    mix = functools.partial(con, "somk,mkco->scmk")
    back = from_spectrum(mix(gr, wr) + mix(gi, wi), mix(gi, wr) - mix(gr, wi))
    point = jnp.einsum("co,soxyz->scxyz", point_weight, dpre, preferred_element_type=f32)
    field_grad = (back + point).astype(bf16)
    outer = functools.partial(con, "scmk,somk->mkco")
    dw = jnp.stack([outer(ur, gr) + outer(ui, gi), outer(ur, gi) - outer(ui, gr)])
    spec_grad = lax.psum(dw, "chan")
    point_part = jnp.einsum("scxyz,soxyz->co", field, dpre, preferred_element_type=f32)
    bias_part = jnp.sum(dpre.astype(f32), axis=(0, 2, 3, 4))
    point_part, bias_part = lax.psum((point_part, bias_part), ("slab", "chan"))
    scale = 1.0 / math.sqrt(samples * lax.axis_size("chan") * NX * NY * NZ)
    return field_grad, spec_grad, point_part * scale, bias_part * scale


def solution(mesh):
    ns, nchan = mesh.shape["slab"], mesh.shape["chan"]

    def per_device(field, *rest):
        samples, _, rows, _, _ = field.shape
        if MY % ns == 0 and rows % (2 * GROUP) == 0 and samples == 1:
            return fast_device(ns, nchan, field, *rest)
        return plain_device(field, *rest)

    return jax.shard_map(
        per_device,
        mesh=mesh,
        in_specs=(
            P(("groups", "chan"), None, "slab", None, None),
            P(("groups", "chan"), None, "slab", None, None),
            P(None, None, "slab", None, None),
            P(),
            P(),
        ),
        out_specs=(
            P(("groups", "chan"), None, "slab", None, None),
            P("groups", None, "slab", None, None),
            P("groups", None),
            P("groups"),
        ),
        check_vma=False,
    )
```

```python
import functools
import math

import jax
import jax.numpy as jnp
import numpy as np
from jax import lax
from jax.experimental import pallas as pl
from jax.experimental.pallas import tpu as pltpu
from jax.sharding import PartitionSpec as P

NX = 128
NY = 128
NZ = 128
MX = 16
MY = 16
MZ = 8
LANES = 128
GROUP = 8

FIELD_CB = 8
PAD = 8
ROWS = 4
GRAD_CB = 4

f32 = jnp.float32
bf16 = jnp.bfloat16

GA = 0.7978845608
GB = 0.044715
GK = (GA * GB) ** (1.0 / 3.0)
GALPHA = GA / GK
SLOPE = 1.5

SCALE_FORWARD = 1.0 / math.sqrt(NX * NY * NZ)
SCALE_INVERSE = 1.0 / math.sqrt(MX * MY * MZ)


def mode_table(length, count, signed):
    position = np.arange(length)[:, None]
    index = np.arange(count)[None, :]
    frequency = np.where(index >= count // 2, index - count, index) if signed else index
    angle = (position * frequency % length).astype(np.float64) * (2.0 * math.pi / length)
    return np.cos(angle).astype(np.float32), (-np.sin(angle)).astype(np.float32)


def bf(value):
    return np.asarray(value, np.float32).astype(jnp.bfloat16)


def split_bf(value):
    high = bf(value)
    return high, bf(np.asarray(value, np.float32) - high.astype(np.float32))


def z_forward_table():
    zc, zs = mode_table(NZ, MZ, False)
    block = np.concatenate([zc, zs], axis=1)
    table = np.zeros((GROUP, NZ, GROUP, 2 * MZ), np.float32)
    for x in range(GROUP):
        table[x, :, x] = block
    return bf(table.reshape(GROUP * NZ, GROUP * 2 * MZ))


def z_inverse_table():
    zc, zs = mode_table(NZ, MZ, False)
    block = np.concatenate([zc, zs], axis=1).T
    table = np.zeros((GROUP // 2, GROUP, 2 * MZ, 2, NZ), np.float32)
    for x in range(GROUP):
        table[x // 2, x, :, x % 2] = block
    return bf(table.reshape(GROUP // 2, GROUP * 2 * MZ, 2 * NZ))


def y_tables():
    yc, ys = mode_table(NY, MY, True)
    forward = np.concatenate([yc.T, ys.T], axis=0)
    inverse = np.concatenate([yc, ys, yc, ys], axis=1)
    return bf(forward), bf(inverse)


def x_forward_table(scale):
    xc, xs = mode_table(NX, MX, True)
    table = np.zeros((NX, 2, MZ, 2, MX, MZ), np.float32)
    for kz in range(MZ):
        table[:, 0, kz, 0, :, kz] = xc
        table[:, 1, kz, 0, :, kz] = -xs
        table[:, 0, kz, 1, :, kz] = xs
        table[:, 1, kz, 1, :, kz] = xc
    return table.reshape(NX * 2 * MZ, 2 * MX * MZ) * (scale * SCALE_FORWARD)


def x_inverse_table(scale, ns):
    xc, xs = mode_table(NX, MX, True)
    table = np.zeros((2, MX, MZ, 2, NX, 2, MZ), np.float32)
    for kz in range(MZ):
        re_re, im_re = xc.T, xs.T
        re_im, im_im = -xs.T, xc.T
        table[0, :, kz, 0, :, 0, kz] = re_re
        table[1, :, kz, 0, :, 0, kz] = im_re
        table[0, :, kz, 0, :, 1, kz] = re_im
        table[1, :, kz, 0, :, 1, kz] = im_im
        table[0, :, kz, 1, :, 0, kz] = re_im
        table[1, :, kz, 1, :, 0, kz] = im_im
        table[0, :, kz, 1, :, 1, kz] = -re_re
        table[1, :, kz, 1, :, 1, kz] = -im_re
    table = table.reshape(2 * MX * MZ, 2, ns, NX // ns * 2 * MZ).transpose(2, 0, 1, 3)
    return table.reshape(ns, 2 * MX * MZ, -1) * scale


def dot(a, b):
    return jnp.dot(a, b, preferred_element_type=f32)


def parts(value):
    high = value.astype(bf16)
    return high, (value - high.astype(f32)).astype(bf16)


def dot3(a, bh, bl):
    ah, al = parts(a)
    return dot(ah, bh) + dot(al, bh) + dot(ah, bl)


def z_forward(tiles, zf):
    wide = jnp.concatenate(
        [
            jnp.concatenate(tiles[g : g + GROUP], axis=1)
            for g in range(0, len(tiles), GROUP)
        ],
        axis=0,
    )
    q = dot(wide, zf).astype(bf16)
    return [q[g : g + NY] for g in range(0, q.shape[0], NY)]


def y_forward(groups, yf):
    r = dot(yf, jnp.concatenate(groups, axis=1))
    top, bot = r[:MY], r[MY:]
    lanes = bot.shape[1]
    at = lax.broadcasted_iota(jnp.int32, top.shape, 1) % (2 * MZ)
    return jnp.where(
        at < MZ, top - pltpu.roll(bot, lanes - MZ, 1), top + pltpu.roll(bot, MZ, 1)
    )


def x_forward_out(me, ns, channels, r_scr, xfh, xfl, outs):
    rows = (MY // ns) * channels
    r = jnp.concatenate([r_scr[i] for i in range(r_scr.shape[0])], axis=1)
    width = xfh.shape[1]
    done = dot3(r, xfh[...], xfl[...])
    for i in range(width // LANES):
        r_scr[i] = done[:, i * LANES : (i + 1) * LANES]
    for k in range(ns):
        owner = lax.rem(me + k, ns)
        at = pl.ds(pl.multiple_of(owner * rows, rows), rows)
        for i in range(width // LANES):
            outs[k][:, :, i * LANES : (i + 1) * LANES] = r_scr[i, at, :].reshape(
                MY // ns, channels, LANES
            )


def x_inverse_in(me, ns, channels, ins, xih, xil, b_scr):
    rows = (MY // ns) * channels
    h = jnp.concatenate([ref[...].reshape(rows, -1) for ref in ins], axis=0)
    b = dot3(h, xih[0], xil[0])
    for k in range(ns):
        owner = lax.rem(me + ns - k, ns)
        at = pl.ds(pl.multiple_of(owner * rows, rows), rows)
        for i in range(b_scr.shape[0]):
            b_scr[i, at, :] = b[k * rows : (k + 1) * rows, i * LANES : (i + 1) * LANES]


def put_channel(scr, c, channels, value):
    for i in range(scr.shape[0]):
        scr[i, pl.ds(c, MY, stride=channels), :] = value[:, i * LANES : (i + 1) * LANES]


def get_channel(scr, c, channels, blocks):
    return jnp.concatenate(
        [scr[i, pl.ds(c, MY, stride=channels), :] for i in blocks], axis=1
    )


def y_inverse(bs, yi):
    lanes = bs[0].shape[1] // 2
    rhs = []
    for b in bs:
        high, low = parts(b)
        rhs.append(
            jnp.concatenate(
                [high[:, :lanes], high[:, lanes:], low[:, :lanes], low[:, lanes:]], axis=0
            )
        )
    return dot(yi, jnp.concatenate(rhs, axis=1)).astype(bf16)


def kron_halves(block):
    channels, _, lanes = block.shape
    wide = block.astype(f32).reshape(channels, 2, 8, lanes)
    return [wide[:, h].reshape(channels * 8, lanes).astype(bf16) for h in range(2)]


def row_pair(ref, x, y):
    return jnp.concatenate([ref[0, :, x + i, y : y + 16, :] for i in range(2)], axis=2)


def whole_rows(value, at, lanes):
    size = value.shape[0] // 8
    two = [value[:, a : a + lanes].reshape(size, 8, lanes) for a in (at, at + lanes)]
    return jnp.concatenate(two, axis=1)


def put_rows(ref, x, y, value):
    value = value.astype(bf16)
    ref[0, :, x, y : y + 16, :] = value[:, :, :NZ]
    ref[0, :, x + 1, y : y + 16, :] = value[:, :, NZ:]


def pick_rows(channels):
    row = lax.broadcasted_iota(jnp.int32, (channels * 8, channels), 0)
    col = lax.broadcasted_iota(jnp.int32, (channels * 8, channels), 1)
    return row // 8 == col


def same_cell(channels):
    size = channels * 8
    row = lax.broadcasted_iota(jnp.int32, (size, size), 0)
    col = lax.broadcasted_iota(jnp.int32, (size, size), 1)
    return row % 8 == col % 8


def kron_rows(point, turned):
    channels = point.shape[0]
    pick = jnp.where(pick_rows(channels), 1.0, 0.0).astype(bf16)
    nt = (((1,), (1,)), ((), ()))
    tn = (((1,), (0,)), ((), ()))
    left = lax.dot_general(pick, point, nt if turned else tn, preferred_element_type=f32)
    full = lax.dot_general(left.astype(bf16), pick, nt, preferred_element_type=f32)
    return jnp.where(same_cell(channels), full, 0.0).astype(bf16)


def field_kernel(ns, channels, me_ref, field, zf, yf, xfh, xfl, *rest):
    outs, r_scr = rest[:ns], rest[ns]
    step = pl.program_id(0)
    rows = field.shape[2]
    lanes = rows * 2 * MZ
    groups = []
    for i in range(FIELD_CB):
        groups += z_forward([field[0, i, x] for x in range(rows)], zf[...])
    spectra = y_forward(groups, yf[...])
    for i in range(FIELD_CB):
        put_channel(r_scr, step * FIELD_CB + i, channels, spectra[:, i * lanes : (i + 1) * lanes])

    @pl.when(step == pl.num_programs(0) - 1)
    def _():
        x_forward_out(me_ref[0], ns, channels, r_scr, xfh, xfl, outs)


def point_kernel(field, point, bias, out, kron):
    channels = field.shape[1]

    @pl.when(pl.program_id(0) == 0)
    def _():
        kron[...] = kron_rows(point[...], True)

    bias_rows = jnp.sum(jnp.where(pick_rows(channels), bias[...], 0.0), axis=1, keepdims=True) * GK
    bias_16 = jnp.concatenate([bias_rows.reshape(channels, 8, 1)] * 2, axis=1)

    for x in range(0, field.shape[2], 2):
        halves = []
        for y in range(0, NY, 16):
            halves += kron_halves(row_pair(field, x, y))
        lanes = halves[0].shape[1]
        done = dot(kron[...], jnp.concatenate(halves, axis=1))
        for y in range(0, NY, 16):
            put_rows(out, x, y, whole_rows(done, y // 8 * lanes, lanes) * GK + bias_16)


def gelu_slope(v):
    n = v * v
    t = jnp.tanh(v * (n + GALPHA))
    return (1.0 + t) * (0.5 / SLOPE + (1.0 - t) * (v * (n + GALPHA / 3.0)))


def grad_kernel(ns, channels, me_ref, pre, cot, *rest):
    ins = rest[:ns]
    xih, xil, yi, zi, zf, yf, xfh, xfl = rest[ns : ns + 8]
    dpre = rest[ns + 8]
    outs = rest[ns + 9 : ns + 9 + ns]
    b_scr, r_scr = rest[ns + 9 + ns :]
    step = pl.program_id(0)
    rows = pre.shape[2]
    width = GROUP * 2 * MZ
    groups = rows // GROUP

    @pl.when(step == 0)
    def _():
        x_inverse_in(me_ref[0], ns, channels, ins, xih, xil, b_scr)

    lanes = rows * 2 * MZ
    blocks = range(b_scr.shape[0])
    wide = y_inverse(
        [get_channel(b_scr, step * GRAD_CB + i, channels, blocks) for i in range(GRAD_CB)], yi[...]
    )
    pairs = GROUP // 2

    def inverse(i, j):
        first = i * groups * width
        rows_of = [wide[:, first + g * width : first + (g + 1) * width] for g in range(groups)]
        point = [
            jnp.concatenate([pre[0, i, g * GROUP + 2 * j + h] for h in range(2)], axis=1)
            for g in range(groups)
        ]
        both = [jnp.concatenate(point, axis=0), jnp.concatenate(rows_of, axis=0)]
        return dot(jnp.concatenate(both, axis=1), zi[j])

    def slope(i, j, v_all):
        for g in range(groups):
            x = g * GROUP + 2 * j
            v = v_all[g * NY : (g + 1) * NY]
            w = jnp.concatenate([cot[0, i, x], cot[0, i, x + 1]], axis=1)
            d = (w.astype(f32) * gelu_slope(v)).astype(bf16)
            dpre[0, i, x] = d[:, :NZ]
            dpre[0, i, x + 1] = d[:, NZ:]

    done = []
    for i in range(GRAD_CB + 1):
        for j in range(pairs):
            if i < GRAD_CB:
                slope(i, j, inverse(i, j))
            if i and j == 0:
                done += z_forward([dpre[0, i - 1, x] for x in range(rows)], zf[...])
    spectra = y_forward(done, yf[...])
    for i in range(GRAD_CB):
        put_channel(r_scr, step * GRAD_CB + i, channels, spectra[:, i * lanes : (i + 1) * lanes])

    @pl.when(step == pl.num_programs(0) - 1)
    def _():
        x_forward_out(me_ref[0], ns, channels, r_scr, xfh, xfl, outs)


def pair_kernel(field, dpre, out, acc):
    channels = field.shape[1]
    step = pl.program_id(0)

    @pl.when(step == 0)
    def _():
        acc[...] = jnp.zeros_like(acc)

    for x in range(0, field.shape[2], 2):
        lefts, rights = [], []
        for y in range(0, NY, 16):
            lefts += kron_halves(row_pair(field, x, y))
            rights += kron_halves(row_pair(dpre, x, y))
        acc[...] += lax.dot_general(
            jnp.concatenate(lefts, axis=1),
            jnp.concatenate(rights, axis=1),
            (((1,), (1,)), ((), ())),
            preferred_element_type=f32,
        )

    @pl.when(step == pl.num_programs(0) - 1)
    def _():
        same = jnp.where(same_cell(channels), acc[...], 0.0)
        pick = jnp.where(pick_rows(channels), 1.0, 0.0)
        high = lax.Precision.HIGHEST
        left = jnp.dot(same, pick, precision=high, preferred_element_type=f32)
        out[...] = lax.dot_general(
            pick, left, (((0,), (0,)), ((), ())), precision=high, preferred_element_type=f32
        ) * SLOPE


def back_kernel(ns, me_ref, dpre, point, *rest):
    ins = rest[:ns]
    xih, xil, yi, zi = rest[ns : ns + 4]
    out, b_scr, g_scr, kron = rest[ns + 4 :]
    channels = dpre.shape[1]
    step = pl.program_id(0)
    width = GROUP * 2 * MZ

    @pl.when(step == 0)
    def _():
        x_inverse_in(me_ref[0], ns, channels, ins, xih, xil, b_scr)
        kron[...] = kron_rows(point[...], False)

    per_group = GROUP // dpre.shape[2]

    @pl.when(step % per_group == 0)
    def _():
        group = step // per_group
        turned = group + b_scr.shape[0] // 2
        wide = y_inverse(
            [get_channel(b_scr, c, channels, (group, turned)) for c in range(channels)], yi[...]
        )
        for c in range(channels):
            g_scr[c] = wide[:, c * width : (c + 1) * width]

    flat = g_scr[...].reshape(channels * NY, width)
    pairs = dpre.shape[2] // 2
    for p in range(pairs):
        x = 2 * p
        halves = []
        for y in range(0, NY, 16):
            halves += kron_halves(row_pair(dpre, x, y))
        lanes = halves[0].shape[1]
        point = dot(kron[...], jnp.concatenate(halves, axis=1))
        spec = dot(flat, zi[step % per_group * pairs + p]).reshape(channels, NY, lanes)
        for y in range(0, NY, 16):
            one = whole_rows(point, y // 8 * lanes, lanes) * SLOPE
            put_rows(out, x, y, one + spec[:, y : y + 16])


def mix_kernel(ns, adjoint, *refs):
    ins, weights, total, out = refs[:ns], refs[ns], refs[ns + 1], refs[ns + 2]
    rows, channels, width = total.shape
    half = width // 2
    u = ins[0][...]
    for k in range(1, ns):
        u = u + ins[k][...]
    total[...] = u
    for ky in range(rows):
        if not adjoint:
            real = jnp.zeros((channels, half), f32)
            imag = jnp.zeros((channels, half), f32)
            for c in range(channels):
                a, b = total[ky, pl.ds(c, 1), :half], total[ky, pl.ds(c, 1), half:]
                wr, wi = weights[0, c, ky].astype(f32), weights[1, c, ky].astype(f32)
                real = real + (wr * a - wi * b)
                imag = imag + (wr * b + wi * a)
            out[ky, :, :half] = real
            out[ky, :, half:] = imag
        else:
            a, b = total[ky, :, :half], total[ky, :, half:]
            for c in range(channels):
                wr, wi = weights[0, c, ky].astype(f32), weights[1, c, ky].astype(f32)
                out[ky, pl.ds(c, 1), :half] = jnp.sum(wr * a + wi * b, axis=0, keepdims=True)
                out[ky, pl.ds(c, 1), half:] = jnp.sum(wr * b - wi * a, axis=0, keepdims=True)


def weight_kernel(weights, out, scr):
    _, kxs, kzs, channels, _ = weights.shape
    modes = kxs * kzs
    stride = channels + PAD
    wide = weights[...].astype(f32).reshape(modes, channels, channels)
    scr[:, :channels, :channels] = wide
    flat = scr.reshape(modes * stride, LANES)
    per = LANES // channels
    lane = lax.broadcasted_iota(jnp.int32, (modes, LANES), 1) // channels
    for c in range(0, channels, per):
        packed = flat[pl.ds(c, modes, stride=stride), :]
        for q in range(1, per):
            more = flat[pl.ds(c + q, modes, stride=stride), :]
            packed = jnp.where(lane == q, pltpu.roll(more, q * channels, 1), packed)
        turned = packed.T.astype(bf16)
        for q in range(per):
            out[0, c + q, 0] = turned[q * channels : (q + 1) * channels]


def outer_kernel(samples, *refs):
    us, gs, out, scr = refs[:samples], refs[samples : 2 * samples], refs[-2], refs[-1]
    channels = us[0].shape[1]
    modes = us[0].shape[2] // 2
    per = LANES // channels
    tn = (((0,), (0,)), ((), ()))

    def stack(refs):
        wide = jnp.concatenate([ref[0] for ref in refs], axis=1)
        return jnp.concatenate(parts(wide), axis=0)

    def table(lanes, of):
        row = lax.broadcasted_iota(jnp.int32, (2 * channels, lanes), 0) % channels
        col = lax.broadcasted_iota(jnp.int32, (2 * channels, lanes), 1)
        return jnp.where(row == of(col), 1.0, 0.0).astype(bf16)

    stride = channels + PAD
    flat = scr.reshape(2, modes * stride, LANES)
    by_o = table(LANES, lambda col: col % channels)
    by_c = table(channels * channels, lambda col: col // channels)
    g_all = lax.dot_general(stack(gs), by_o, tn, preferred_element_type=f32)
    u_all = lax.dot_general(stack(us), by_c, tn, preferred_element_type=f32)
    for n in range(channels // per):
        real = imag = None
        for s in range(samples):
            at = 2 * s * modes
            gr, gi = g_all[at : at + modes], g_all[at + modes : at + 2 * modes]
            u = u_all[at : at + 2 * modes, n * LANES : (n + 1) * LANES]
            ur, ui = u[:modes], u[modes:]
            re, im = ur * gr + ui * gi, ur * gi - ui * gr
            real = re if real is None else real + re
            imag = im if imag is None else imag + im
        for p, value in enumerate((real, imag)):
            for q in range(per):
                one = value if q == 0 else pltpu.roll(value, LANES - q * channels, 1)
                flat[p, pl.ds(n * per + q, modes, stride=stride), :] = one
    out[...] = scr[:, :, :channels, :channels].reshape(out.shape)


def whole(shape):
    return pl.BlockSpec(shape, lambda *_: (0,) * len(shape))


def params(mib=60, axes=1):
    return pltpu.CompilerParams(
        dimension_semantics=("arbitrary",) * axes, vmem_limit_bytes=mib * 2**20
    )


def make_calls(ns, shape):
    _, channels, rows, _, _ = shape
    own_ky = MY // ns
    width = 2 * MX * MZ
    lanes = rows * 2 * MZ
    size = channels * 8

    zf = jnp.asarray(z_forward_table())
    zi = jnp.asarray(z_inverse_table())
    same = np.broadcast_to(bf(np.eye(2 * NZ)), (GROUP // 2, 2 * NZ, 2 * NZ))
    zi_pre = jnp.asarray(np.concatenate([same, z_inverse_table()], axis=1))
    yf, yi = (jnp.asarray(t) for t in y_tables())
    xf = [jnp.asarray(t) for t in split_bf(x_forward_table(1.0))]
    xf_grad = [jnp.asarray(t) for t in split_bf(x_forward_table(SLOPE))]
    xf_spec = [pl.BlockSpec((lanes, width), lambda i, at: (at[0], 0))] * 2
    xi_pre = [jnp.asarray(t) for t in split_bf(x_inverse_table(SCALE_INVERSE * GK, ns))]
    xi_back = [jnp.asarray(t) for t in split_bf(x_inverse_table(SCALE_INVERSE, ns))]
    xi_spec = [pl.BlockSpec((1, width, 2 * lanes), lambda i, at: (at[0], 0, 0))] * 2

    chunk = jax.ShapeDtypeStruct((own_ky, channels, width), f32)
    chunk_spec = whole(chunk.shape)

    def some_channels(count):
        return pl.BlockSpec((1, count, rows, NY, NZ), lambda c, *_: (0, c, 0, 0, 0))

    some_rows = pl.BlockSpec((1, channels, ROWS, NY, NZ), lambda x, *_: (0, 0, x, 0, 0))
    big = jax.ShapeDtypeStruct(shape, bf16)
    cells = channels * rows * NY * NZ
    r_scr = pltpu.VMEM((lanes // LANES, MY * channels, LANES), f32)
    b_scr = pltpu.VMEM((2 * lanes // LANES, MY * channels, LANES), f32)
    kron_scr = pltpu.VMEM((size, size), bf16)

    def cost(flops, moved):
        return pl.CostEstimate(flops=int(flops), bytes_accessed=int(moved), transcendentals=0)

    def tables(*arrays):
        return [whole(a.shape) for a in arrays]

    def field_call(me_arr, field):
        return pl.pallas_call(
            functools.partial(field_kernel, ns, channels),
            grid_spec=pltpu.PrefetchScalarGridSpec(
                num_scalar_prefetch=1,
                grid=(channels // FIELD_CB,),
                in_specs=[some_channels(FIELD_CB)] + tables(zf, yf) + xf_spec,
                out_specs=[chunk_spec] * ns,
                scratch_shapes=[r_scr],
            ),
            out_shape=[chunk] * ns,
            compiler_params=params(),
            cost_estimate=cost(cells * 512, cells * 2),
            name="field_spectrum",
        )(me_arr, field, zf, yf, *xf)

    def point_call(field, point_weight, bias):
        return pl.pallas_call(
            point_kernel,
            grid=(rows // ROWS,),
            in_specs=[some_rows] + tables(point_weight, bias[None]),
            out_specs=some_rows,
            out_shape=big,
            scratch_shapes=[kron_scr],
            compiler_params=params(),
            cost_estimate=cost(cells * 512, cells * 4),
            name="pointwise",
        )(field, point_weight, bias[None])

    def mix_call(adjoint, chunks, w):
        return pl.pallas_call(
            functools.partial(mix_kernel, ns, adjoint),
            grid=(1,),
            in_specs=[chunk_spec] * ns + tables(w),
            out_specs=[chunk_spec, chunk_spec],
            out_shape=[chunk, chunk],
            compiler_params=params(),
            name="mix_adjoint" if adjoint else "mix",
        )(*chunks, w)

    def grad_call(me_arr, pre, cotangent, chunks):
        return pl.pallas_call(
            functools.partial(grad_kernel, ns, channels),
            grid_spec=pltpu.PrefetchScalarGridSpec(
                num_scalar_prefetch=1,
                grid=(channels // GRAD_CB,),
                in_specs=[some_channels(GRAD_CB)] * 2
                + [chunk_spec] * ns
                + xi_spec
                + tables(yi, zi_pre, zf, yf)
                + xf_spec,
                out_specs=[some_channels(GRAD_CB)] + [chunk_spec] * ns,
                scratch_shapes=[b_scr, r_scr],
            ),
            out_shape=[big] + [chunk] * ns,
            compiler_params=params(),
            cost_estimate=cost(cells * 1024, cells * 6),
            name="gelu_gradient",
        )(me_arr, pre, cotangent, *chunks, *xi_pre, yi, zi_pre, zf, yf, *xf_grad)

    def pair_call(field, dpre, part=0, count=1):
        steps = rows // ROWS // count
        part_rows = pl.BlockSpec(
            (1, channels, ROWS, NY, NZ), lambda x: (0, 0, x + part * steps, 0, 0)
        )
        return pl.pallas_call(
            pair_kernel,
            grid=(steps,),
            in_specs=[part_rows, part_rows],
            out_specs=whole((channels, channels)),
            out_shape=jax.ShapeDtypeStruct((channels, channels), f32),
            scratch_shapes=[pltpu.VMEM((size, size), f32)],
            compiler_params=params(),
            cost_estimate=cost(cells * 512 // count, cells * 4 // count),
            name="point_gradient",
        )(field, dpre)

    def back_call(me_arr, dpre, point_weight, chunks):
        return pl.pallas_call(
            functools.partial(back_kernel, ns),
            grid_spec=pltpu.PrefetchScalarGridSpec(
                num_scalar_prefetch=1,
                grid=(rows // ROWS,),
                in_specs=[some_rows]
                + tables(point_weight)
                + [chunk_spec] * ns
                + xi_spec
                + tables(yi, zi),
                out_specs=some_rows,
                scratch_shapes=[b_scr, pltpu.VMEM((channels, NY, GROUP * 2 * MZ), bf16), kron_scr],
            ),
            out_shape=big,
            compiler_params=params(),
            cost_estimate=cost(cells * 1024, cells * 4),
            name="field_gradient",
        )(me_arr, dpre, point_weight, *chunks, *xi_back, yi, zi)

    modes = MX * MZ
    w_block = pl.BlockSpec((1, MX, MZ, channels, channels), lambda p, k: (p, 0, k, 0, 0))

    def weight_call(spec_weight):
        return pl.pallas_call(
            weight_kernel,
            grid=(2, own_ky),
            in_specs=[w_block],
            out_specs=pl.BlockSpec(
                (1, channels, 1, channels, modes), lambda p, k: (p, 0, k, 0, 0)
            ),
            out_shape=jax.ShapeDtypeStruct((2, channels, own_ky, channels, modes), bf16),
            scratch_shapes=[pltpu.VMEM((modes, channels + PAD, LANES), f32)],
            compiler_params=params(axes=2),
            cost_estimate=cost(0, 2 * own_ky * modes * channels * LANES * 2),
            name="weight_layout",
        )(spec_weight)

    def spec_call(every):
        one_u = pl.BlockSpec((1, channels, width), lambda k: (k, 0, 0))
        one_g = pl.BlockSpec((1, channels, width), lambda k: (own_ky + k, 0, 0))
        return pl.pallas_call(
            functools.partial(outer_kernel, len(every)),
            grid=(own_ky,),
            in_specs=[one_u] * len(every) + [one_g] * len(every),
            out_specs=pl.BlockSpec((2, MX, MZ, channels, channels), lambda k: (0, 0, k, 0, 0)),
            out_shape=jax.ShapeDtypeStruct((2, MX, own_ky * MZ, channels, channels), f32),
            scratch_shapes=[pltpu.VMEM((2, modes, channels + PAD, LANES), f32)],
            compiler_params=params(),
            cost_estimate=cost(0, 2 * own_ky * modes * channels * LANES * 4),
            name="weight_gradient",
        )(*every, *every)

    return {
        "field": field_call,
        "point": point_call,
        "mix": mix_call,
        "grad": grad_call,
        "pair": pair_call,
        "back": back_call,
        "weights": weight_call,
        "spec": spec_call,
    }


def fast_device(ns, nchan, field, cotangent, spec_weight, point_weight, bias):
    channels = field.shape[1]
    me = lax.axis_index("slab")
    me_arr = me[None].astype(jnp.int32)
    calls = make_calls(ns, field.shape)

    def swap(chunks, axis, size):
        got = [chunks[0]]
        for k in range(1, size):
            pairs = [(i, (i + k) % size) for i in range(size)]
            got.append(lax.ppermute(chunks[k], axis, pairs))
        return got

    field_chunks = calls["field"](me_arr, field)
    w = calls["weights"](spec_weight)
    pre = calls["point"](field, point_weight, bias)
    uhat, vhat = calls["mix"](False, swap(field_chunks, "slab", ns), w)
    vhats = swap([vhat] * ns, "slab", ns)
    dpre, *grad_chunks = calls["grad"](me_arr, pre, cotangent, vhats)

    point_part = calls["pair"](field, dpre, 0, 2)
    ghat, hhat = calls["mix"](True, swap(grad_chunks, "slab", ns), w)
    hhats = swap([hhat] * ns, "slab", ns)
    dpre_later, _ = lax.optimization_barrier((dpre, hhat))
    point_part = point_part + calls["pair"](field, dpre_later, 1, 2)

    norm_scale = 1.0 / math.sqrt(nchan * NX * NY * NZ)
    dc = jnp.where(me == 0, ghat[0, :, 0], 0.0) * (1.0 / SCALE_FORWARD)
    tail = jnp.concatenate([point_part, dc[:, None]], axis=1)
    tail = jnp.pad(tail, ((0, 0), (0, ghat.shape[2] - tail.shape[1])))
    sample = jnp.concatenate([uhat, ghat, tail[None]], axis=0)
    every = swap([sample] * nchan, "chan", nchan)
    field_grad = calls["back"](me_arr, dpre, point_weight, hhats)
    every, field_grad = lax.optimization_barrier((every, field_grad))
    tails = swap([sum(one[-1, :, : channels + 1] for one in every)] * ns, "slab", ns)

    spec_grad = calls["spec"](every)
    tail = sum(tails) * norm_scale
    return field_grad, spec_grad, tail[:, :channels], tail[:, channels]


def plain_device(field, cotangent, spec_weight, point_weight, bias):
    samples, channels, rows, _, _ = field.shape
    high = lax.Precision.HIGHEST

    def con(form, a, b):
        return jnp.einsum(form, a, b, precision=high)

    yc, ys = (jnp.asarray(t) for t in mode_table(NY, MY, True))
    zc, zs = (jnp.asarray(t) for t in mode_table(NZ, MZ, False))
    xc, xs = (jnp.asarray(t) for t in mode_table(NX, MX, True))
    y_table = jnp.concatenate([yc, ys], axis=1).astype(bf16)
    z_table = jnp.concatenate([zc, zs], axis=1)
    pairs = MY * MZ

    def to_spectrum(values):
        q = jnp.einsum("scxyz,yk->scxkz", values, y_table, preferred_element_type=f32)
        zr = con("scxkz,zj->scxkj", q[:, :, :, :MY], z_table)
        zm = con("scxkz,zj->scxkj", q[:, :, :, MY:], z_table)
        real = zr[..., :MZ] - zm[..., MZ:]
        imag = zr[..., MZ:] + zm[..., :MZ]
        local = jnp.stack([real, imag]).reshape(2, samples, channels, rows, pairs)
        a, b = lax.all_to_all(local, "slab", split_axis=4, concat_axis=3, tiled=True)
        real = con("scxk,xm->scmk", a, xc) - con("scxk,xm->scmk", b, xs)
        imag = con("scxk,xm->scmk", b, xc) + con("scxk,xm->scmk", a, xs)
        return real * SCALE_FORWARD, imag * SCALE_FORWARD

    def from_spectrum(a, b):
        real = con("scmk,xm->scxk", a, xc) + con("scmk,xm->scxk", b, xs)
        imag = con("scmk,xm->scxk", b, xc) - con("scmk,xm->scxk", a, xs)
        both = jnp.stack([real, imag])
        both = lax.all_to_all(both, "slab", split_axis=3, concat_axis=4, tiled=True)
        real, imag = both.reshape(2, samples, channels, rows, MY, MZ)
        fr = con("scxkj,zj->scxkz", real, zc) + con("scxkj,zj->scxkz", imag, zs)
        fi = con("scxkj,zj->scxkz", imag, zc) - con("scxkj,zj->scxkz", real, zs)
        f = jnp.concatenate([fr, fi], axis=3).astype(bf16)
        out = jnp.einsum("scxkz,yk->scxyz", f, y_table, preferred_element_type=f32)
        return out * SCALE_INVERSE

    wr, wi = spec_weight.astype(f32)
    ur, ui = to_spectrum(field)
    mix = functools.partial(con, "scmk,mkco->somk")
    spectral = from_spectrum(mix(ur, wr) - mix(ui, wi), mix(ui, wr) + mix(ur, wi))
    point = jnp.einsum("co,scxyz->soxyz", point_weight, field, preferred_element_type=f32)
    pre = (spectral + point + bias[None, :, None, None, None]) * GK
    dpre = (cotangent.astype(f32) * gelu_slope(pre)).astype(bf16)
    gr, gi = to_spectrum(dpre)
    mix = functools.partial(con, "somk,mkco->scmk")
    back = from_spectrum(mix(gr, wr) + mix(gi, wi), mix(gi, wr) - mix(gr, wi))
    point = jnp.einsum("co,soxyz->scxyz", point_weight, dpre, preferred_element_type=f32)
    field_grad = (back + point).astype(bf16)
    outer = functools.partial(con, "scmk,somk->mkco")
    dw = jnp.stack([outer(ur, gr) + outer(ui, gi), outer(ur, gi) - outer(ui, gr)])
    spec_grad = lax.psum(dw, "chan")
    point_part = jnp.einsum("scxyz,soxyz->co", field, dpre, preferred_element_type=f32)
    bias_part = jnp.sum(dpre.astype(f32), axis=(0, 2, 3, 4))
    point_part, bias_part = lax.psum((point_part, bias_part), ("slab", "chan"))
    scale = 1.0 / math.sqrt(samples * lax.axis_size("chan") * NX * NY * NZ)
    return field_grad, spec_grad, point_part * scale, bias_part * scale


def solution(mesh):
    ns, nchan = mesh.shape["slab"], mesh.shape["chan"]

    def per_device(field, *rest):
        samples, _, rows, _, _ = field.shape
        if MY % ns == 0 and rows % (2 * GROUP) == 0 and samples == 1:
            return fast_device(ns, nchan, field, *rest)
        return plain_device(field, *rest)

    return jax.shard_map(
        per_device,
        mesh=mesh,
        in_specs=(
            P(("groups", "chan"), None, "slab", None, None),
            P(("groups", "chan"), None, "slab", None, None),
            P(None, None, "slab", None, None),
            P(),
            P(),
        ),
        out_specs=(
            P(("groups", "chan"), None, "slab", None, None),
            P("groups", None, "slab", None, None),
            P("groups", None),
            P("groups"),
        ),
        check_vma=False,
    )
```

```python
import functools
import math

import jax
import jax.numpy as jnp
import numpy as np
from jax import lax
from jax.experimental import pallas as pl
from jax.experimental.pallas import tpu as pltpu
from jax.sharding import PartitionSpec as P

NX = 128
NY = 128
NZ = 128
MX = 16
MY = 16
MZ = 8
LANES = 128
GROUP = 8

FIELD_CB = 8
PAD = 8
ROWS = 8
PAIR_ROWS = 4
GRAD_CB = 4

f32 = jnp.float32
bf16 = jnp.bfloat16

GA = 0.7978845608
GB = 0.044715
GK = (GA * GB) ** (1.0 / 3.0)
GALPHA = GA / GK
SLOPE = 1.5

SCALE_FORWARD = 1.0 / math.sqrt(NX * NY * NZ)
SCALE_INVERSE = 1.0 / math.sqrt(MX * MY * MZ)


def mode_table(length, count, signed):
    position = np.arange(length)[:, None]
    index = np.arange(count)[None, :]
    frequency = np.where(index >= count // 2, index - count, index) if signed else index
    angle = (position * frequency % length).astype(np.float64) * (2.0 * math.pi / length)
    return np.cos(angle).astype(np.float32), (-np.sin(angle)).astype(np.float32)


def bf(value):
    return np.asarray(value, np.float32).astype(jnp.bfloat16)


def split_bf(value):
    high = bf(value)
    return high, bf(np.asarray(value, np.float32) - high.astype(np.float32))


def z_forward_table():
    zc, zs = mode_table(NZ, MZ, False)
    block = np.concatenate([zc, zs], axis=1)
    table = np.zeros((GROUP, NZ, GROUP, 2 * MZ), np.float32)
    for x in range(GROUP):
        table[x, :, x] = block
    return bf(table.reshape(GROUP * NZ, GROUP * 2 * MZ))


def z_inverse_table():
    zc, zs = mode_table(NZ, MZ, False)
    block = np.concatenate([zc, zs], axis=1).T
    table = np.zeros((GROUP // 2, GROUP, 2 * MZ, 2, NZ), np.float32)
    for x in range(GROUP):
        table[x // 2, x, :, x % 2] = block
    return bf(table.reshape(GROUP // 2, GROUP * 2 * MZ, 2 * NZ))


def y_tables():
    yc, ys = mode_table(NY, MY, True)
    forward = np.concatenate([yc.T, ys.T], axis=0)
    inverse = np.concatenate([yc, ys, yc, ys], axis=1)
    return bf(forward), bf(inverse)


def x_forward_table(scale):
    xc, xs = mode_table(NX, MX, True)
    table = np.zeros((NX, 2, MZ, 2, MX, MZ), np.float32)
    for kz in range(MZ):
        table[:, 0, kz, 0, :, kz] = xc
        table[:, 1, kz, 0, :, kz] = -xs
        table[:, 0, kz, 1, :, kz] = xs
        table[:, 1, kz, 1, :, kz] = xc
    return table.reshape(NX * 2 * MZ, 2 * MX * MZ) * (scale * SCALE_FORWARD)


def x_inverse_table(scale, ns):
    xc, xs = mode_table(NX, MX, True)
    table = np.zeros((2, MX, MZ, 2, NX, 2, MZ), np.float32)
    for kz in range(MZ):
        re_re, im_re = xc.T, xs.T
        re_im, im_im = -xs.T, xc.T
        table[0, :, kz, 0, :, 0, kz] = re_re
        table[1, :, kz, 0, :, 0, kz] = im_re
        table[0, :, kz, 0, :, 1, kz] = re_im
        table[1, :, kz, 0, :, 1, kz] = im_im
        table[0, :, kz, 1, :, 0, kz] = re_im
        table[1, :, kz, 1, :, 0, kz] = im_im
        table[0, :, kz, 1, :, 1, kz] = -re_re
        table[1, :, kz, 1, :, 1, kz] = -im_re
    table = table.reshape(2 * MX * MZ, 2, ns, NX // ns * 2 * MZ).transpose(2, 0, 1, 3)
    return table.reshape(ns, 2 * MX * MZ, -1) * scale


def dot(a, b):
    return jnp.dot(a, b, preferred_element_type=f32)


def parts(value):
    high = value.astype(bf16)
    return high, (value - high.astype(f32)).astype(bf16)


def dot3(a, bh, bl):
    ah, al = parts(a)
    return dot(ah, bh) + dot(al, bh) + dot(ah, bl)


def z_forward(tiles, zf):
    wide = jnp.concatenate(
        [
            jnp.concatenate(tiles[g : g + GROUP], axis=1)
            for g in range(0, len(tiles), GROUP)
        ],
        axis=0,
    )
    q = dot(wide, zf).astype(bf16)
    return [q[g : g + NY] for g in range(0, q.shape[0], NY)]


def y_forward(groups, yf):
    r = dot(yf, jnp.concatenate(groups, axis=1))
    top, bot = r[:MY], r[MY:]
    lanes = bot.shape[1]
    at = lax.broadcasted_iota(jnp.int32, top.shape, 1) % (2 * MZ)
    return jnp.where(
        at < MZ, top - pltpu.roll(bot, lanes - MZ, 1), top + pltpu.roll(bot, MZ, 1)
    )


def x_forward_out(me, ns, channels, r_scr, xfh, xfl, outs):
    rows = (MY // ns) * channels
    r = jnp.concatenate([r_scr[i] for i in range(r_scr.shape[0])], axis=1)
    width = xfh.shape[1]
    done = dot3(r, xfh[...], xfl[...])
    for i in range(width // LANES):
        r_scr[i] = done[:, i * LANES : (i + 1) * LANES]
    for k in range(ns):
        owner = lax.rem(me + k, ns)
        at = pl.ds(pl.multiple_of(owner * rows, rows), rows)
        for i in range(width // LANES):
            outs[k][:, :, i * LANES : (i + 1) * LANES] = r_scr[i, at, :].reshape(
                MY // ns, channels, LANES
            )


def x_inverse_in(me, ns, channels, ins, xih, xil, b_scr):
    rows = (MY // ns) * channels
    h = jnp.concatenate([ref[...].reshape(rows, -1) for ref in ins], axis=0)
    b = dot3(h, xih[0], xil[0])
    for k in range(ns):
        owner = lax.rem(me + ns - k, ns)
        at = pl.ds(pl.multiple_of(owner * rows, rows), rows)
        for i in range(b_scr.shape[0]):
            b_scr[i, at, :] = b[k * rows : (k + 1) * rows, i * LANES : (i + 1) * LANES]


def put_channel(scr, c, channels, value):
    for i in range(scr.shape[0]):
        scr[i, pl.ds(c, MY, stride=channels), :] = value[:, i * LANES : (i + 1) * LANES]


def get_channel(scr, c, channels, blocks):
    return jnp.concatenate(
        [scr[i, pl.ds(c, MY, stride=channels), :] for i in blocks], axis=1
    )


def y_inverse(bs, yi):
    lanes = bs[0].shape[1] // 2
    rhs = []
    for b in bs:
        high, low = parts(b)
        rhs.append(
            jnp.concatenate(
                [high[:, :lanes], high[:, lanes:], low[:, :lanes], low[:, lanes:]], axis=0
            )
        )
    return dot(yi, jnp.concatenate(rhs, axis=1)).astype(bf16)


def kron_halves(block):
    channels, _, lanes = block.shape
    wide = block.astype(f32).reshape(channels, 2, 8, lanes)
    return [wide[:, h].reshape(channels * 8, lanes).astype(bf16) for h in range(2)]


def row_pair(ref, x, y):
    return jnp.concatenate([ref[0, :, x + i, y : y + 16, :] for i in range(2)], axis=2)


def whole_rows(value, at, lanes):
    size = value.shape[0] // 8
    two = [value[:, a : a + lanes].reshape(size, 8, lanes) for a in (at, at + lanes)]
    return jnp.concatenate(two, axis=1)


def put_rows(ref, x, y, value):
    value = value.astype(bf16)
    ref[0, :, x, y : y + 16, :] = value[:, :, :NZ]
    ref[0, :, x + 1, y : y + 16, :] = value[:, :, NZ:]


def pick_rows(channels):
    row = lax.broadcasted_iota(jnp.int32, (channels * 8, channels), 0)
    col = lax.broadcasted_iota(jnp.int32, (channels * 8, channels), 1)
    return row // 8 == col


def same_cell(channels):
    size = channels * 8
    row = lax.broadcasted_iota(jnp.int32, (size, size), 0)
    col = lax.broadcasted_iota(jnp.int32, (size, size), 1)
    return row % 8 == col % 8


def kron_rows(point, turned):
    channels = point.shape[0]
    pick = jnp.where(pick_rows(channels), 1.0, 0.0).astype(bf16)
    nt = (((1,), (1,)), ((), ()))
    tn = (((1,), (0,)), ((), ()))
    left = lax.dot_general(pick, point, nt if turned else tn, preferred_element_type=f32)
    full = lax.dot_general(left.astype(bf16), pick, nt, preferred_element_type=f32)
    return jnp.where(same_cell(channels), full, 0.0).astype(bf16)


def field_kernel(ns, channels, me_ref, field, zf, yf, xfh, xfl, *rest):
    outs, r_scr = rest[:ns], rest[ns]
    step = pl.program_id(0)
    rows = field.shape[2]
    lanes = rows * 2 * MZ
    groups = []
    for i in range(FIELD_CB):
        groups += z_forward([field[0, i, x] for x in range(rows)], zf[...])
    spectra = y_forward(groups, yf[...])
    for i in range(FIELD_CB):
        put_channel(r_scr, step * FIELD_CB + i, channels, spectra[:, i * lanes : (i + 1) * lanes])

    @pl.when(step == pl.num_programs(0) - 1)
    def _():
        x_forward_out(me_ref[0], ns, channels, r_scr, xfh, xfl, outs)


def point_kernel(field, point, bias, out, kron):
    channels = field.shape[1]

    @pl.when(pl.program_id(0) == 0)
    def _():
        kron[...] = kron_rows(point[...], True)

    bias_rows = jnp.sum(jnp.where(pick_rows(channels), bias[...], 0.0), axis=1, keepdims=True) * GK
    bias_16 = jnp.concatenate([bias_rows.reshape(channels, 8, 1)] * 2, axis=1)

    for x in range(0, field.shape[2], 2):
        halves = []
        for y in range(0, NY, 16):
            halves += kron_halves(row_pair(field, x, y))
        lanes = halves[0].shape[1]
        done = dot(kron[...], jnp.concatenate(halves, axis=1))
        for y in range(0, NY, 16):
            put_rows(out, x, y, whole_rows(done, y // 8 * lanes, lanes) * GK + bias_16)


def gelu_slope(v):
    n = v * v
    t = jnp.tanh(v * (n + GALPHA))
    return (1.0 + t) * (0.5 / SLOPE + (1.0 - t) * (v * (n + GALPHA / 3.0)))


def grad_kernel(ns, channels, me_ref, pre, cot, *rest):
    ins = rest[:ns]
    xih, xil, yi, zi, zf, yf, xfh, xfl = rest[ns : ns + 8]
    dpre = rest[ns + 8]
    outs = rest[ns + 9 : ns + 9 + ns]
    b_scr, r_scr = rest[ns + 9 + ns :]
    step = pl.program_id(0)
    rows = pre.shape[2]
    width = GROUP * 2 * MZ
    groups = rows // GROUP

    @pl.when(step == 0)
    def _():
        x_inverse_in(me_ref[0], ns, channels, ins, xih, xil, b_scr)

    lanes = rows * 2 * MZ
    blocks = range(b_scr.shape[0])
    wide = y_inverse(
        [get_channel(b_scr, step * GRAD_CB + i, channels, blocks) for i in range(GRAD_CB)], yi[...]
    )
    pairs = GROUP // 2

    def inverse(i, j, part):
        both = []
        for g in part:
            at = (i * groups + g) * width
            x = g * GROUP + 2 * j
            both.append(
                jnp.concatenate([pre[0, i, x], pre[0, i, x + 1], wide[:, at : at + width]], axis=1)
            )
        return dot(jnp.concatenate(both, axis=0), zi[j])

    def slope(i, j, part, v_all):
        for n, g in enumerate(part):
            x = g * GROUP + 2 * j
            v = v_all[n * NY : (n + 1) * NY]
            w = jnp.concatenate([cot[0, i, x], cot[0, i, x + 1]], axis=1)
            d = (w.astype(f32) * gelu_slope(v)).astype(bf16)
            dpre[0, i, x] = d[:, :NZ]
            dpre[0, i, x + 1] = d[:, NZ:]

    together = 1
    done = []
    for i in range(GRAD_CB + 1):
        for j in range(pairs):
            if i < GRAD_CB:
                for g in range(0, groups, together):
                    part = range(g, g + together)
                    slope(i, j, part, inverse(i, j, part))
            if i and j == 0:
                done += z_forward([dpre[0, i - 1, x] for x in range(rows)], zf[...])
    spectra = y_forward(done, yf[...])
    for i in range(GRAD_CB):
        put_channel(r_scr, step * GRAD_CB + i, channels, spectra[:, i * lanes : (i + 1) * lanes])

    @pl.when(step == pl.num_programs(0) - 1)
    def _():
        x_forward_out(me_ref[0], ns, channels, r_scr, xfh, xfl, outs)


def pair_kernel(field, dpre, out, acc):
    channels = field.shape[1]
    step = pl.program_id(0)

    @pl.when(step == 0)
    def _():
        acc[...] = jnp.zeros_like(acc)

    for x in range(0, field.shape[2], 2):
        lefts, rights = [], []
        for y in range(0, NY, 16):
            lefts += kron_halves(row_pair(field, x, y))
            rights += kron_halves(row_pair(dpre, x, y))
        acc[...] += lax.dot_general(
            jnp.concatenate(lefts, axis=1),
            jnp.concatenate(rights, axis=1),
            (((1,), (1,)), ((), ())),
            preferred_element_type=f32,
        )

    @pl.when(step == pl.num_programs(0) - 1)
    def _():
        same = jnp.where(same_cell(channels), acc[...], 0.0)
        pick = jnp.where(pick_rows(channels), 1.0, 0.0)
        high = lax.Precision.HIGHEST
        left = jnp.dot(same, pick, precision=high, preferred_element_type=f32)
        out[...] = lax.dot_general(
            pick, left, (((0,), (0,)), ((), ())), precision=high, preferred_element_type=f32
        ) * SLOPE


def back_kernel(ns, me_ref, dpre, point, *rest):
    ins = rest[:ns]
    xih, xil, yi, zi = rest[ns : ns + 4]
    out, b_scr, g_scr, kron = rest[ns + 4 :]
    channels = dpre.shape[1]
    step = pl.program_id(0)
    width = GROUP * 2 * MZ

    @pl.when(step == 0)
    def _():
        x_inverse_in(me_ref[0], ns, channels, ins, xih, xil, b_scr)
        kron[...] = kron_rows(point[...], False)

    per_group = GROUP // dpre.shape[2]

    @pl.when(step % per_group == 0)
    def _():
        group = step // per_group
        turned = group + b_scr.shape[0] // 2
        wide = y_inverse(
            [get_channel(b_scr, c, channels, (group, turned)) for c in range(channels)], yi[...]
        )
        for c in range(channels):
            g_scr[c] = wide[:, c * width : (c + 1) * width]

    flat = g_scr[...].reshape(channels * NY, width)
    pairs = dpre.shape[2] // 2
    for p in range(pairs):
        x = 2 * p
        halves = []
        for y in range(0, NY, 16):
            halves += kron_halves(row_pair(dpre, x, y))
        lanes = halves[0].shape[1]
        point = dot(kron[...], jnp.concatenate(halves, axis=1))
        spec = dot(flat, zi[step % per_group * pairs + p]).reshape(channels, NY, lanes)
        for y in range(0, NY, 16):
            one = whole_rows(point, y // 8 * lanes, lanes) * SLOPE
            put_rows(out, x, y, one + spec[:, y : y + 16])


def mix_kernel(ns, adjoint, *refs):
    ins, weights, total, out = refs[:ns], refs[ns], refs[ns + 1], refs[ns + 2]
    rows, channels, width = total.shape
    half = width // 2
    u = ins[0][...]
    for k in range(1, ns):
        u = u + ins[k][...]
    total[...] = u
    for ky in range(rows):
        if not adjoint:
            real = jnp.zeros((channels, half), f32)
            imag = jnp.zeros((channels, half), f32)
            for c in range(channels):
                a, b = total[ky, pl.ds(c, 1), :half], total[ky, pl.ds(c, 1), half:]
                wr, wi = weights[0, c, ky].astype(f32), weights[1, c, ky].astype(f32)
                real = real + (wr * a - wi * b)
                imag = imag + (wr * b + wi * a)
            out[ky, :, :half] = real
            out[ky, :, half:] = imag
        else:
            a, b = total[ky, :, :half], total[ky, :, half:]
            for c in range(channels):
                wr, wi = weights[0, c, ky].astype(f32), weights[1, c, ky].astype(f32)
                out[ky, pl.ds(c, 1), :half] = jnp.sum(wr * a + wi * b, axis=0, keepdims=True)
                out[ky, pl.ds(c, 1), half:] = jnp.sum(wr * b - wi * a, axis=0, keepdims=True)


def weight_kernel(weights, out, scr):
    _, kxs, kzs, channels, _ = weights.shape
    modes = kxs * kzs
    stride = channels + PAD
    wide = weights[...].astype(f32).reshape(modes, channels, channels)
    scr[:, :channels, :channels] = wide
    flat = scr.reshape(modes * stride, LANES)
    per = LANES // channels
    lane = lax.broadcasted_iota(jnp.int32, (modes, LANES), 1) // channels
    for c in range(0, channels, per):
        packed = flat[pl.ds(c, modes, stride=stride), :]
        for q in range(1, per):
            more = flat[pl.ds(c + q, modes, stride=stride), :]
            packed = jnp.where(lane == q, pltpu.roll(more, q * channels, 1), packed)
        turned = packed.T.astype(bf16)
        for q in range(per):
            out[0, c + q, 0] = turned[q * channels : (q + 1) * channels]


def outer_kernel(samples, *refs):
    us, gs, out, scr = refs[:samples], refs[samples : 2 * samples], refs[-2], refs[-1]
    channels = us[0].shape[1]
    modes = us[0].shape[2] // 2
    per = LANES // channels
    tn = (((0,), (0,)), ((), ()))

    def stack(refs):
        wide = jnp.concatenate([ref[0] for ref in refs], axis=1)
        return jnp.concatenate(parts(wide), axis=0)

    def table(lanes, of):
        row = lax.broadcasted_iota(jnp.int32, (2 * channels, lanes), 0) % channels
        col = lax.broadcasted_iota(jnp.int32, (2 * channels, lanes), 1)
        return jnp.where(row == of(col), 1.0, 0.0).astype(bf16)

    stride = channels + PAD
    flat = scr.reshape(2, modes * stride, LANES)
    by_o = table(LANES, lambda col: col % channels)
    by_c = table(channels * channels, lambda col: col // channels)
    g_all = lax.dot_general(stack(gs), by_o, tn, preferred_element_type=f32)
    u_all = lax.dot_general(stack(us), by_c, tn, preferred_element_type=f32)
    for n in range(channels // per):
        real = imag = None
        for s in range(samples):
            at = 2 * s * modes
            gr, gi = g_all[at : at + modes], g_all[at + modes : at + 2 * modes]
            u = u_all[at : at + 2 * modes, n * LANES : (n + 1) * LANES]
            ur, ui = u[:modes], u[modes:]
            re, im = ur * gr + ui * gi, ur * gi - ui * gr
            real = re if real is None else real + re
            imag = im if imag is None else imag + im
        for p, value in enumerate((real, imag)):
            for q in range(per):
                one = value if q == 0 else pltpu.roll(value, LANES - q * channels, 1)
                flat[p, pl.ds(n * per + q, modes, stride=stride), :] = one
    out[...] = scr[:, :, :channels, :channels].reshape(out.shape)


def whole(shape):
    return pl.BlockSpec(shape, lambda *_: (0,) * len(shape))


def params(mib=60, axes=1):
    return pltpu.CompilerParams(
        dimension_semantics=("arbitrary",) * axes, vmem_limit_bytes=mib * 2**20
    )


def make_calls(ns, shape):
    _, channels, rows, _, _ = shape
    own_ky = MY // ns
    width = 2 * MX * MZ
    lanes = rows * 2 * MZ
    size = channels * 8

    zf = jnp.asarray(z_forward_table())
    zi = jnp.asarray(z_inverse_table())
    same = np.broadcast_to(bf(np.eye(2 * NZ)), (GROUP // 2, 2 * NZ, 2 * NZ))
    zi_pre = jnp.asarray(np.concatenate([same, z_inverse_table()], axis=1))
    yf, yi = (jnp.asarray(t) for t in y_tables())
    xf = [jnp.asarray(t) for t in split_bf(x_forward_table(1.0))]
    xf_grad = [jnp.asarray(t) for t in split_bf(x_forward_table(SLOPE))]
    xf_spec = [pl.BlockSpec((lanes, width), lambda i, at: (at[0], 0))] * 2
    xi_pre = [jnp.asarray(t) for t in split_bf(x_inverse_table(SCALE_INVERSE * GK, ns))]
    xi_back = [jnp.asarray(t) for t in split_bf(x_inverse_table(SCALE_INVERSE, ns))]
    xi_spec = [pl.BlockSpec((1, width, 2 * lanes), lambda i, at: (at[0], 0, 0))] * 2

    chunk = jax.ShapeDtypeStruct((own_ky, channels, width), f32)
    chunk_spec = whole(chunk.shape)

    def some_channels(count):
        return pl.BlockSpec((1, count, rows, NY, NZ), lambda c, *_: (0, c, 0, 0, 0))

    some_rows = pl.BlockSpec((1, channels, ROWS, NY, NZ), lambda x, *_: (0, 0, x, 0, 0))
    big = jax.ShapeDtypeStruct(shape, bf16)
    cells = channels * rows * NY * NZ
    r_scr = pltpu.VMEM((lanes // LANES, MY * channels, LANES), f32)
    b_scr = pltpu.VMEM((2 * lanes // LANES, MY * channels, LANES), f32)
    kron_scr = pltpu.VMEM((size, size), bf16)

    def cost(flops, moved):
        return pl.CostEstimate(flops=int(flops), bytes_accessed=int(moved), transcendentals=0)

    def tables(*arrays):
        return [whole(a.shape) for a in arrays]

    def field_call(me_arr, field):
        return pl.pallas_call(
            functools.partial(field_kernel, ns, channels),
            grid_spec=pltpu.PrefetchScalarGridSpec(
                num_scalar_prefetch=1,
                grid=(channels // FIELD_CB,),
                in_specs=[some_channels(FIELD_CB)] + tables(zf, yf) + xf_spec,
                out_specs=[chunk_spec] * ns,
                scratch_shapes=[r_scr],
            ),
            out_shape=[chunk] * ns,
            compiler_params=params(),
            cost_estimate=cost(cells * 512, cells * 2),
            name="field_spectrum",
        )(me_arr, field, zf, yf, *xf)

    def point_call(field, point_weight, bias):
        return pl.pallas_call(
            point_kernel,
            grid=(rows // ROWS,),
            in_specs=[some_rows] + tables(point_weight, bias[None]),
            out_specs=some_rows,
            out_shape=big,
            scratch_shapes=[kron_scr],
            compiler_params=params(),
            cost_estimate=cost(cells * 512, cells * 4),
            name="pointwise",
        )(field, point_weight, bias[None])

    def mix_call(adjoint, chunks, w):
        return pl.pallas_call(
            functools.partial(mix_kernel, ns, adjoint),
            grid=(1,),
            in_specs=[chunk_spec] * ns + tables(w),
            out_specs=[chunk_spec, chunk_spec],
            out_shape=[chunk, chunk],
            compiler_params=params(),
            name="mix_adjoint" if adjoint else "mix",
        )(*chunks, w)

    def grad_call(me_arr, pre, cotangent, chunks):
        return pl.pallas_call(
            functools.partial(grad_kernel, ns, channels),
            grid_spec=pltpu.PrefetchScalarGridSpec(
                num_scalar_prefetch=1,
                grid=(channels // GRAD_CB,),
                in_specs=[some_channels(GRAD_CB)] * 2
                + [chunk_spec] * ns
                + xi_spec
                + tables(yi, zi_pre, zf, yf)
                + xf_spec,
                out_specs=[some_channels(GRAD_CB)] + [chunk_spec] * ns,
                scratch_shapes=[b_scr, r_scr],
            ),
            out_shape=[big] + [chunk] * ns,
            compiler_params=params(),
            cost_estimate=cost(cells * 1024, cells * 6),
            name="gelu_gradient",
        )(me_arr, pre, cotangent, *chunks, *xi_pre, yi, zi_pre, zf, yf, *xf_grad)

    def pair_call(field, dpre, part=0, count=1):
        steps = rows // PAIR_ROWS // count
        part_rows = pl.BlockSpec(
            (1, channels, PAIR_ROWS, NY, NZ), lambda x: (0, 0, x + part * steps, 0, 0)
        )
        return pl.pallas_call(
            pair_kernel,
            grid=(steps,),
            in_specs=[part_rows, part_rows],
            out_specs=whole((channels, channels)),
            out_shape=jax.ShapeDtypeStruct((channels, channels), f32),
            scratch_shapes=[pltpu.VMEM((size, size), f32)],
            compiler_params=params(),
            cost_estimate=cost(cells * 512 // count, cells * 4 // count),
            name="point_gradient",
        )(field, dpre)

    def back_call(me_arr, dpre, point_weight, chunks):
        return pl.pallas_call(
            functools.partial(back_kernel, ns),
            grid_spec=pltpu.PrefetchScalarGridSpec(
                num_scalar_prefetch=1,
                grid=(rows // ROWS,),
                in_specs=[some_rows]
                + tables(point_weight)
                + [chunk_spec] * ns
                + xi_spec
                + tables(yi, zi),
                out_specs=some_rows,
                scratch_shapes=[b_scr, pltpu.VMEM((channels, NY, GROUP * 2 * MZ), bf16), kron_scr],
            ),
            out_shape=big,
            compiler_params=params(),
            cost_estimate=cost(cells * 1024, cells * 4),
            name="field_gradient",
        )(me_arr, dpre, point_weight, *chunks, *xi_back, yi, zi)

    modes = MX * MZ
    w_block = pl.BlockSpec((1, MX, MZ, channels, channels), lambda p, k: (p, 0, k, 0, 0))

    def weight_call(spec_weight):
        return pl.pallas_call(
            weight_kernel,
            grid=(2, own_ky),
            in_specs=[w_block],
            out_specs=pl.BlockSpec(
                (1, channels, 1, channels, modes), lambda p, k: (p, 0, k, 0, 0)
            ),
            out_shape=jax.ShapeDtypeStruct((2, channels, own_ky, channels, modes), bf16),
            scratch_shapes=[pltpu.VMEM((modes, channels + PAD, LANES), f32)],
            compiler_params=params(axes=2),
            cost_estimate=cost(0, 2 * own_ky * modes * channels * LANES * 2),
            name="weight_layout",
        )(spec_weight)

    def spec_call(every):
        one_u = pl.BlockSpec((1, channels, width), lambda k: (k, 0, 0))
        one_g = pl.BlockSpec((1, channels, width), lambda k: (own_ky + k, 0, 0))
        return pl.pallas_call(
            functools.partial(outer_kernel, len(every)),
            grid=(own_ky,),
            in_specs=[one_u] * len(every) + [one_g] * len(every),
            out_specs=pl.BlockSpec((2, MX, MZ, channels, channels), lambda k: (0, 0, k, 0, 0)),
            out_shape=jax.ShapeDtypeStruct((2, MX, own_ky * MZ, channels, channels), f32),
            scratch_shapes=[pltpu.VMEM((2, modes, channels + PAD, LANES), f32)],
            compiler_params=params(),
            cost_estimate=cost(0, 2 * own_ky * modes * channels * LANES * 4),
            name="weight_gradient",
        )(*every, *every)

    return {
        "field": field_call,
        "point": point_call,
        "mix": mix_call,
        "grad": grad_call,
        "pair": pair_call,
        "back": back_call,
        "weights": weight_call,
        "spec": spec_call,
    }


def fast_device(ns, nchan, field, cotangent, spec_weight, point_weight, bias):
    channels = field.shape[1]
    me = lax.axis_index("slab")
    me_arr = me[None].astype(jnp.int32)
    calls = make_calls(ns, field.shape)

    def swap(chunks, axis, size):
        got = [chunks[0]]
        for k in range(1, size):
            pairs = [(i, (i + k) % size) for i in range(size)]
            got.append(lax.ppermute(chunks[k], axis, pairs))
        return got

    field_chunks = calls["field"](me_arr, field)
    w = calls["weights"](spec_weight)
    pre = calls["point"](field, point_weight, bias)
    uhat, vhat = calls["mix"](False, swap(field_chunks, "slab", ns), w)
    vhats = swap([vhat] * ns, "slab", ns)
    dpre, *grad_chunks = calls["grad"](me_arr, pre, cotangent, vhats)

    point_part = calls["pair"](field, dpre, 0, 2)
    ghat, hhat = calls["mix"](True, swap(grad_chunks, "slab", ns), w)
    hhats = swap([hhat] * ns, "slab", ns)
    dpre_later, _ = lax.optimization_barrier((dpre, hhat))
    point_part = point_part + calls["pair"](field, dpre_later, 1, 2)

    norm_scale = 1.0 / math.sqrt(nchan * NX * NY * NZ)
    dc = jnp.where(me == 0, ghat[0, :, 0], 0.0) * (1.0 / SCALE_FORWARD)
    tail = jnp.concatenate([point_part, dc[:, None]], axis=1)
    tail = jnp.pad(tail, ((0, 0), (0, ghat.shape[2] - tail.shape[1])))
    sample = jnp.concatenate([uhat, ghat, tail[None]], axis=0)
    every = swap([sample] * nchan, "chan", nchan)
    field_grad = calls["back"](me_arr, dpre, point_weight, hhats)
    every, field_grad = lax.optimization_barrier((every, field_grad))
    tails = swap([sum(one[-1, :, : channels + 1] for one in every)] * ns, "slab", ns)

    spec_grad = calls["spec"](every)
    tail = sum(tails) * norm_scale
    return field_grad, spec_grad, tail[:, :channels], tail[:, channels]


def plain_device(field, cotangent, spec_weight, point_weight, bias):
    samples, channels, rows, _, _ = field.shape
    high = lax.Precision.HIGHEST

    def con(form, a, b):
        return jnp.einsum(form, a, b, precision=high)

    yc, ys = (jnp.asarray(t) for t in mode_table(NY, MY, True))
    zc, zs = (jnp.asarray(t) for t in mode_table(NZ, MZ, False))
    xc, xs = (jnp.asarray(t) for t in mode_table(NX, MX, True))
    y_table = jnp.concatenate([yc, ys], axis=1).astype(bf16)
    z_table = jnp.concatenate([zc, zs], axis=1)
    pairs = MY * MZ

    def to_spectrum(values):
        q = jnp.einsum("scxyz,yk->scxkz", values, y_table, preferred_element_type=f32)
        zr = con("scxkz,zj->scxkj", q[:, :, :, :MY], z_table)
        zm = con("scxkz,zj->scxkj", q[:, :, :, MY:], z_table)
        real = zr[..., :MZ] - zm[..., MZ:]
        imag = zr[..., MZ:] + zm[..., :MZ]
        local = jnp.stack([real, imag]).reshape(2, samples, channels, rows, pairs)
        a, b = lax.all_to_all(local, "slab", split_axis=4, concat_axis=3, tiled=True)
        real = con("scxk,xm->scmk", a, xc) - con("scxk,xm->scmk", b, xs)
        imag = con("scxk,xm->scmk", b, xc) + con("scxk,xm->scmk", a, xs)
        return real * SCALE_FORWARD, imag * SCALE_FORWARD

    def from_spectrum(a, b):
        real = con("scmk,xm->scxk", a, xc) + con("scmk,xm->scxk", b, xs)
        imag = con("scmk,xm->scxk", b, xc) - con("scmk,xm->scxk", a, xs)
        both = jnp.stack([real, imag])
        both = lax.all_to_all(both, "slab", split_axis=3, concat_axis=4, tiled=True)
        real, imag = both.reshape(2, samples, channels, rows, MY, MZ)
        fr = con("scxkj,zj->scxkz", real, zc) + con("scxkj,zj->scxkz", imag, zs)
        fi = con("scxkj,zj->scxkz", imag, zc) - con("scxkj,zj->scxkz", real, zs)
        f = jnp.concatenate([fr, fi], axis=3).astype(bf16)
        out = jnp.einsum("scxkz,yk->scxyz", f, y_table, preferred_element_type=f32)
        return out * SCALE_INVERSE

    wr, wi = spec_weight.astype(f32)
    ur, ui = to_spectrum(field)
    mix = functools.partial(con, "scmk,mkco->somk")
    spectral = from_spectrum(mix(ur, wr) - mix(ui, wi), mix(ui, wr) + mix(ur, wi))
    point = jnp.einsum("co,scxyz->soxyz", point_weight, field, preferred_element_type=f32)
    pre = (spectral + point + bias[None, :, None, None, None]) * GK
    dpre = (cotangent.astype(f32) * gelu_slope(pre)).astype(bf16)
    gr, gi = to_spectrum(dpre)
    mix = functools.partial(con, "somk,mkco->scmk")
    back = from_spectrum(mix(gr, wr) + mix(gi, wi), mix(gi, wr) - mix(gr, wi))
    point = jnp.einsum("co,soxyz->scxyz", point_weight, dpre, preferred_element_type=f32)
    field_grad = (back + point).astype(bf16)
    outer = functools.partial(con, "scmk,somk->mkco")
    dw = jnp.stack([outer(ur, gr) + outer(ui, gi), outer(ur, gi) - outer(ui, gr)])
    spec_grad = lax.psum(dw, "chan")
    point_part = jnp.einsum("scxyz,soxyz->co", field, dpre, preferred_element_type=f32)
    bias_part = jnp.sum(dpre.astype(f32), axis=(0, 2, 3, 4))
    point_part, bias_part = lax.psum((point_part, bias_part), ("slab", "chan"))
    scale = 1.0 / math.sqrt(samples * lax.axis_size("chan") * NX * NY * NZ)
    return field_grad, spec_grad, point_part * scale, bias_part * scale


def solution(mesh):
    ns, nchan = mesh.shape["slab"], mesh.shape["chan"]

    def per_device(field, *rest):
        samples, _, rows, _, _ = field.shape
        if MY % ns == 0 and rows % (2 * GROUP) == 0 and samples == 1:
            return fast_device(ns, nchan, field, *rest)
        return plain_device(field, *rest)

    return jax.shard_map(
        per_device,
        mesh=mesh,
        in_specs=(
            P(("groups", "chan"), None, "slab", None, None),
            P(("groups", "chan"), None, "slab", None, None),
            P(None, None, "slab", None, None),
            P(),
            P(),
        ),
        out_specs=(
            P(("groups", "chan"), None, "slab", None, None),
            P("groups", None, "slab", None, None),
            P("groups", None),
            P("groups"),
        ),
        check_vma=False,
    )
```
